128 devices in a mesh: prompt: 8 (over z, core), comp: 16 (over y, x).
Axes of the slice: x: 4, y: 4, z: 4, core: 2. Of those that a mesh axis runs over, the one named last changes fastest.
Arguments:
- queries: bfloat16 [512, 3, 8192], P(('prompt', 'comp')), may hold values from -98 to 98
- new_kv: bfloat16 [512, 3, 2, 512], P(('prompt', 'comp')), may hold values from -8 to 8
- suffix_kv: bfloat16 [512, 256, 2, 512], P(('prompt', 'comp')), may hold values from -8 to 8
- suffix_len: int32 [512], P(('prompt', 'comp')), may hold values from 1 to 256
- pool_kv: bfloat16 [1024, 128, 2, 512], P(('prompt', 'comp')), may hold values from -8 to 8
- sys_kv: bfloat16 [2048, 2, 512], P(('prompt', 'comp')), may hold values from -8 to 8
- block_slot: int32 [8, 128], P('prompt'), may hold values from 0 to 127, as said below
- block_list: int32 [512, 64], P(('prompt', 'comp')), may hold values from 0 to 127, as said below
- prefix_blocks: int32 [512], P(('prompt', 'comp')), may hold values from 32 to 64, as said below
Outputs:
- attn_out: bfloat16 [512, 3, 8192], P(('prompt', 'comp'))
The draws below stay inside these ranges and needn't reach their ends.
Inputs may be any that keep to these rules, and one draw needn't show every extreme that they name: `block_slot`: each row is a permutation of the 128 slots of one group; the slots d * 8 to (d + 1) * 8 - 1 hold exactly 4 logical blocks of each prompt's region. `block_list`: the 32 consecutive completions of one prompt share one row; entries of a row are distinct blocks of its prompt's region, blocks p * 64 to (p + 1) * 64 - 1 for prompt p = (c % 64) // 32. `prefix_blocks`: shared by the completions of one prompt; in every group some prompt has 64.
All inputs are finite; a program needn't handle non-finite values.
Results may differ from the reference program's by a relative error of at most 0.0055.
Values may be sent and summed in bfloat16 or wider, within the bound.
No kernel may reach another device: no remote copies, remote signals or barrier semaphores. Data moves between devices by JAX's collectives and lax.ppermute only.
A program may use at most 128 MiB of HBM per device.

```python
import jax
import jax.numpy as jnp
from jax import lax

QH = 64
KVH = 4
HD = 128
BLK = 128
STEPS = 3
PROMPTS = 2
SUF = 256
BLK_DEV = 8
POOL = 128
POOL_ALL = 1024
QMAX = 64
CMPS_G = 64
CPP = 32
CMPS = 512
SYS = 2048
N_PROMPT = 8
N_COMP = 16


def permute_region(subkey):
    return jax.random.permutation(subkey, QMAX)


def permute_device(subkey):
    return jax.random.permutation(subkey, BLK_DEV)


def prompt_tree(key):
    lengths = jax.random.randint(jax.random.fold_in(key, 101), (N_PROMPT, PROMPTS), QMAX // 2, QMAX + 1)
    longest = jax.random.randint(jax.random.fold_in(key, 102), (N_PROMPT,), 0, PROMPTS)
    lengths = jnp.where(jnp.arange(PROMPTS)[None, :] == longest[:, None], QMAX, lengths)
    orders = jax.vmap(permute_region)(jax.random.split(jax.random.fold_in(key, 103), N_PROMPT * PROMPTS))
    orders = orders.reshape(N_PROMPT, PROMPTS, QMAX) + (jnp.arange(PROMPTS) * QMAX)[None, :, None]
    completion = jnp.arange(CMPS)
    group_id = completion // CMPS_G
    prompt_id = completion % CMPS_G // CPP
    return (orders[group_id, prompt_id].astype(jnp.int32), lengths[group_id, prompt_id].astype(jnp.int32))


def draw_block_list(key, part):
    lists, counts = prompt_tree(key)
    return lists


def draw_prefix_blocks(key, part):
    lists, counts = prompt_tree(key)
    return counts


def draw_block_slot(key, part):
    key = jax.random.fold_in(key, 21)
    share = BLK_DEV // PROMPTS
    positions = jax.vmap(permute_device)(jax.random.split(key, N_PROMPT * N_COMP)).reshape(N_PROMPT, N_COMP, BLK_DEV)
    slots = positions + (jnp.arange(N_COMP) * BLK_DEV)[None, :, None]
    slots = slots.reshape(N_PROMPT, N_COMP, PROMPTS, share).transpose(0, 2, 1, 3).reshape(N_PROMPT, PROMPTS, QMAX)
    orders = jax.vmap(permute_region)(jax.random.split(jax.random.fold_in(key, 1), N_PROMPT * PROMPTS))
    orders = orders.reshape(N_PROMPT, PROMPTS, QMAX)
    placed = jnp.take_along_axis(slots, orders, axis=2)
    return placed.reshape(N_PROMPT, POOL).astype(jnp.int32)


def draw_suffix_len(key, part):
    key = jax.random.fold_in(key, 5)
    lengths = jax.random.randint(key, (CMPS,), 1, SUF + 1)
    longest = jax.random.randint(jax.random.fold_in(key, 6), (), 0, CMPS)
    return lengths.at[longest].set(SUF).astype(jnp.int32)


def draw_queries(key, part):
    key = jax.random.fold_in(key, 11)
    base = jax.random.normal(key, (CMPS, STEPS, QH * HD), jnp.float32) * 1.6
    return jnp.clip(base, -8.0, 8.0).astype(jnp.bfloat16)


def block_scale(rng, dims, shards, low, largest):
    def one(position, parts):
        steps = jax.random.uniform(jax.random.fold_in(jax.random.fold_in(rng, 6), position), (parts,), jnp.float32, low / len(shards), largest / len(shards))
        return jnp.repeat(jnp.exp(steps), dims[position] // parts).reshape((-1,) + (1,) * (len(dims) - position - 1))

    loudness = one(*shards[0])
    for cut in shards[1:]:
        loudness = loudness * one(*cut)
    return loudness


def gaussian(rng, dims, spread, most, pieces=(), kind=jnp.bfloat16):
    factor_of = block_scale(rng, dims, pieces, -0.22, 0.18) if pieces else 1.0
    values = jax.random.normal(rng, dims, jnp.float32) * spread * factor_of
    return jnp.minimum(jnp.maximum(values, -most), most).astype(kind)


def setup_inputs(seed: int = 0) -> dict:
    arg_keys = jax.random.split(jax.random.key(seed), 10)
    queries = draw_queries(jax.random.fold_in(arg_keys[9], 71), 0)
    new_kv = gaussian(arg_keys[1], (CMPS, STEPS, 2, KVH * HD), 1.6, 8.0, ((0, 128),))
    suffix_kv = gaussian(arg_keys[2], (CMPS, SUF, 2, KVH * HD), 1.6, 8.0, ((0, 128),))
    suffix_len = draw_suffix_len(jax.random.fold_in(arg_keys[9], 71), 0)
    pool_kv = gaussian(arg_keys[4], (POOL_ALL, BLK, 2, KVH * HD), 1.6, 8.0, ((0, 128),))
    sys_kv = gaussian(arg_keys[5], (SYS, 2, KVH * HD), 1.6, 8.0, ((0, 128),))
    block_slot = draw_block_slot(jax.random.fold_in(arg_keys[9], 71), 0)
    block_list = draw_block_list(jax.random.fold_in(arg_keys[9], 71), 0)
    prefix_blocks = draw_prefix_blocks(jax.random.fold_in(arg_keys[9], 71), 0)
    return {"queries": queries, "new_kv": new_kv, "suffix_kv": suffix_kv, "suffix_len": suffix_len, "pool_kv": pool_kv, "sys_kv": sys_kv, "block_slot": block_slot, "block_list": block_list, "prefix_blocks": prefix_blocks}


def reference(queries, new_kv, suffix_kv, suffix_len, pool_kv, sys_kv, block_slot, block_list, prefix_blocks):
    group_size = QH // KVH
    scaling = HD ** -0.5
    sys_keys = sys_kv[:, 0].reshape(SYS, KVH, HD)
    sys_values = sys_kv[:, 1].reshape(SYS, KVH, HD)

    def one_row(completion):
        group_id = completion // CMPS_G
        slot_ids = (group_id * POOL + jnp.take(block_slot[group_id], block_list[completion])).astype(jnp.int32)
        chosen = jnp.take(pool_kv, slot_ids, axis=0)
        prefix_keys = chosen[:, :, 0].reshape(QMAX * BLK, KVH, HD)
        prefix_values = chosen[:, :, 1].reshape(QMAX * BLK, KVH, HD)
        prefix_live = (jnp.arange(QMAX * BLK, dtype=jnp.int32) // BLK) < prefix_blocks[completion]
        suffix_keys = suffix_kv[completion, :, 0].reshape(SUF, KVH, HD)
        suffix_values = suffix_kv[completion, :, 1].reshape(SUF, KVH, HD)
        suffix_live = jnp.arange(SUF, dtype=jnp.int32) < suffix_len[completion]
        fresh_keys = new_kv[completion, :, 0].reshape(STEPS, KVH, HD)
        fresh_values = new_kv[completion, :, 1].reshape(STEPS, KVH, HD)
        all_keys = jnp.concatenate([sys_keys, prefix_keys, suffix_keys, fresh_keys], axis=0)
        all_values = jnp.concatenate([sys_values, prefix_values, suffix_values, fresh_values], axis=0)
        base_live = jnp.concatenate([jnp.ones((SYS,), bool), prefix_live, suffix_live])
        causal = jnp.arange(STEPS)[None, :] <= jnp.arange(STEPS)[:, None]
        live = jnp.concatenate([jnp.broadcast_to(base_live[None, :], (STEPS, base_live.shape[0])), causal], axis=1)
        query_heads = queries[completion].reshape(STEPS, KVH, group_size, HD)
        scores = jnp.einsum("thgd,nhd->thgn", query_heads.astype(jnp.float32), all_keys.astype(jnp.float32)) * scaling
        scores = jnp.where(live[:, None, None, :], scores, -jnp.inf)
        highest = jnp.max(scores, axis=-1, keepdims=True)
        weights = jnp.exp(scores - highest)
        total = jnp.sum(weights, axis=-1)
        rounded = lax.optimization_barrier(weights.astype(jnp.bfloat16)).astype(jnp.float32)
        output = jnp.einsum("thgn,nhd->thgd", rounded, all_values.astype(jnp.float32)) / total[..., None]
        return output.reshape(STEPS, QH * HD).astype(jnp.bfloat16)

    return lax.map(one_row, jnp.arange(CMPS, dtype=jnp.int32))
```

```python
import functools

import jax
import jax.numpy as jnp
from jax import lax
from jax.experimental import pallas as pl
from jax.experimental.pallas import tpu as pltpu
from jax.sharding import PartitionSpec as P

QH = 64
KVH = 4
HD = 128
GQ = QH // KVH
SIDE = 4
BLK = 128
ROWS = 192
MSG = ROWS + 16
SYS_PART = 32
POOL_TOK = 512
ALL_TOK = 5 * POOL_TOK
AXES = ("prompt", "comp")
FLOOR = -1e30
SCALE2 = HD**-0.5 * 1.4426950408889634
BF = jnp.bfloat16
F32 = jnp.float32
NT = (((1,), (1,)), ((), ()))
PARAMS = pltpu.CompilerParams(vmem_limit_bytes=56 * 2**20)
SMEM = pl.BlockSpec(memory_space=pltpu.SMEM)
VMEM = pl.BlockSpec(memory_space=pltpu.VMEM)


def ring_pairs(prompts, role, step):
    pairs = []
    for p in range(prompts):
        along_x = (p % 2 == 0) == (role == "a")
        for y in range(SIDE):
            for x in range(SIDE):
                ty = y if along_x else (y + step) % SIDE
                tx = (x + step) % SIDE if along_x else x
                base = p * SIDE * SIDE
                pairs.append((base + y * SIDE + x, base + ty * SIDE + tx))
    return pairs


def row_pairs(prompts, step):
    count = SIDE * SIDE
    return [(p * count + c, p * count + (c + step * SIDE) % count) for p in range(prompts) for c in range(count)]


def prompt_pairs(prompts, bit):
    count = SIDE * SIDE
    return [(p * count + c, (p ^ bit) * count + c) for p in range(prompts) for c in range(count)]


def turned(meta_ref, k):
    return lax.rem(meta_ref[2] + k, SIDE)


def query_kernel(meta_ref, q_ref, sys_ref, far_ref, o0, o1, o2, o3, tmp, sys_tmp):
    for k, out in enumerate((o0, o1, o2, o3)):
        head = turned(meta_ref, k)
        for t in range(3):
            for g in range(GQ):
                at = pl.ds(pl.multiple_of((head * GQ + g) * HD, HD), HD)
                tmp[pl.ds(t * 64 + g * 4, 4), :] = q_ref[t, :, at].astype(F32)
        out[pl.ds(0, ROWS), :] = tmp[...].astype(BF)
        lanes = pl.ds(pl.multiple_of(head * HD, HD), HD)
        sys_tmp[pl.ds(0, SYS_PART), :] = sys_ref[:, :, lanes].reshape(SYS_PART, HD).astype(F32)
        sys_tmp[pl.ds(SYS_PART, SYS_PART), :] = far_ref[:, :, lanes].reshape(SYS_PART, HD).astype(F32)
        out[pl.ds(ROWS, SYS_PART), :] = sys_tmp[pl.ds(0, SYS_PART, stride=2), :].astype(BF)
        out[pl.ds(ROWS + SYS_PART, SYS_PART), :] = sys_tmp[pl.ds(1, SYS_PART, stride=2), :].astype(BF)


def stage_kernel(m0, m1, m2, m3, stage_ref, sys_ref):
    for k, msg in enumerate((m0, m1, m2, m3)):
        stage_ref[k] = msg[pl.ds(0, ROWS), :]
        for side in range(2):
            at = pl.ds(k * SYS_PART, SYS_PART)
            sys_ref[0, side, at, :] = msg[pl.ds(ROWS + side * SYS_PART, SYS_PART), :]


def flatten_rows(lse):
    lane = lax.broadcasted_iota(jnp.int32, (BLK, HD), 1)
    row = lax.broadcasted_iota(jnp.int32, (BLK, HD), 0)
    rest = ROWS - BLK
    upper = jnp.sum(jnp.where(lane == row, lse[:BLK], 0.0), axis=0, keepdims=True)
    lower = jnp.sum(jnp.where((lane == row)[:rest], lse[BLK:], 0.0), axis=0, keepdims=True)
    return jnp.concatenate([upper, lower], axis=0)


def pack_flat(flat):
    hi = flat.astype(BF).astype(F32)
    mid = (flat - hi).astype(BF).astype(F32)
    low = flat - hi - mid
    return jnp.concatenate([hi, mid, low, jnp.zeros((10, HD), F32)], axis=0).astype(BF)


def unpack_flat(packed):
    wide = packed.astype(F32)
    return wide[0:2] + wide[2:4] + wide[4:6]


def weigh(flats):
    top = functools.reduce(jnp.maximum, flats)
    weights = [jnp.exp2(one - top) for one in flats]
    total = functools.reduce(jnp.add, weights)
    return [w / total for w in weights], top + jnp.log2(total)


def mix_all(weights, outs):
    flat = [w for group in weights for w in group]
    rows = 2 * len(flat)
    stacked = jnp.concatenate(flat + [jnp.zeros((HD - rows, HD), F32)], axis=0)
    columns = stacked.T
    mixed = []
    n = 0
    for group in outs:
        upper = lower = 0.0
        for one in group:
            upper = upper + columns[:, n : n + 1] * one[:BLK]
            lower = lower + columns[: ROWS - BLK, n + 1 : n + 2] * one[BLK:]
            n += 2
        mixed.append(jnp.concatenate([upper, lower], axis=0))
    return mixed


def main_kernel(meta_ref, code_ref, *refs):
    q_refs, pieces, sys_refs, o_refs, refs = refs[:4], refs[4:8], refs[8:10], refs[10:14], refs[14:]
    kc, vc, bias, q_all, o_all, tmp = refs
    j = pl.program_id(0)

    @pl.when(j == 0)
    def _():
        for n, ref in enumerate(q_refs):
            q_all[n] = ref[...]
        for p in range(2):
            vc[p, :, pl.ds(HD, HD)] = jnp.ones((ALL_TOK, HD), BF)
            for n in range(4):
                at = pl.ds(4 * POOL_TOK + n * BLK, BLK)
                kc[p, at, :] = sys_refs[n // 2][n % 2, 0]
                vc[p, at, pl.ds(0, HD)] = sys_refs[n // 2][n % 2, 1]
                bias[p, 16 + n] = jnp.zeros((8, HD), F32)
        for k, ref in enumerate(pieces):
            held = tmp.at[k % 2]
            held[...] = ref[...].astype(F32)
            n0, n1 = jnp.int32(0), jnp.int32(0)
            for blk in range(8):
                code = code_ref[meta_ref[3 + k] + blk]
                prompt = code // 2
                rank = k * 4 + jnp.minimum(jnp.where(prompt == 0, n0, n1), 3)
                at = pl.ds(pl.multiple_of(rank * BLK, BLK), BLK)
                kc[prompt, at, :] = held[pl.ds(blk * 2 * BLK, BLK, stride=2), :].astype(BF)
                vc[prompt, at, pl.ds(0, HD)] = held[pl.ds(blk * 2 * BLK + 1, BLK, stride=2), :].astype(BF)
                dead = jnp.where(code % 2 == 1, 0.0, FLOOR)
                bias[prompt, rank] = jnp.full((8, HD), dead, F32)
                n0 = n0 + 1 - prompt
                n1 = n1 + prompt

    def prompt_of(k):
        shift = jnp.where(meta_ref[7] == 0, j, k)
        return lax.rem(meta_ref[0] - shift + SIDE, SIDE) // 2

    def scores(k):
        p = prompt_of(k)
        s = lax.dot_general(q_all[j, k], kc[p], NT, preferred_element_type=F32)
        return s + jnp.concatenate([bias[p, n, :1, :] for n in range(20)], axis=1)

    def finish(k, s):
        m = jnp.max(s, axis=1, keepdims=True)
        w = jnp.exp2((s - m) * SCALE2).astype(BF)
        acc = jnp.dot(w, vc[prompt_of(k)], preferred_element_type=F32)
        total = acc[:, HD:]
        o_all[k, pl.ds(0, ROWS), :] = (acc[:, :HD] / total).astype(BF)
        o_all[k, pl.ds(ROWS, 16), :] = pack_flat(flatten_rows(m * SCALE2 + jnp.log2(total)))

    s = scores(0)
    for k in range(SIDE):
        following = scores(k + 1) if k + 1 < SIDE else None
        finish(k, s)
        s = following
    for n, ref in enumerate(o_refs):

        @pl.when(j == n)
        def _():
            ref[...] = o_all[...]


def own_kernel(lens_ref, q0, q1, q2, q3, s0, s1, s2, s3, new_ref, o_ref, lse_ref, bias, tmp, vc):
    tokens = vc.shape[1]
    comp = lax.broadcasted_iota(jnp.int32, (ROWS, 256), 0) % 4
    place = lax.broadcasted_iota(jnp.int32, (ROWS, 256), 1)
    for c in range(4):
        live = (comp == c) & (place < lens_ref[c])
        bias[:, pl.ds(c * 256, 256)] = jnp.where(live, 0.0, FLOOR)
    row = lax.broadcasted_iota(jnp.int32, (ROWS, BLK), 0)
    col = lax.broadcasted_iota(jnp.int32, (ROWS, BLK), 1)
    fresh = col - (row % 4) * 3
    bias[:, pl.ds(1024, BLK)] = jnp.where((fresh >= 0) & (fresh < 3) & (fresh <= row // 64), 0.0, FLOOR)
    for n in range(2):
        vc[n, :, pl.ds(HD, HD)] = jnp.ones((tokens, HD), BF)
        tmp[n, pl.ds(2048, 256), :] = jnp.zeros((256, HD), F32)

    def scores(k, q_ref, kv_ref):
        held = tmp.at[k % 2]
        held[pl.ds(0, 2048), :] = kv_ref[...].astype(F32)
        held[pl.ds(2048, 24), :] = new_ref[k].astype(F32)
        key = held[pl.ds(0, tokens, stride=2), :].astype(BF)
        vc[k % 2, :, pl.ds(0, HD)] = held[pl.ds(1, tokens, stride=2), :].astype(BF)
        s = lax.dot_general(q_ref[pl.ds(0, ROWS), :], key, NT, preferred_element_type=F32)
        return s + bias[...]

    def finish(k, s):
        m = jnp.max(s, axis=1, keepdims=True)
        w = jnp.exp2((s - m) * SCALE2).astype(BF)
        acc = jnp.dot(w, vc[k % 2], preferred_element_type=F32)
        total = acc[:, HD:]
        o_ref[k] = acc[:, :HD] / total
        lse_ref[k, pl.ds(0, 2), :] = flatten_rows(m * SCALE2 + jnp.log2(total))

    q_refs, kv_refs = (q0, q1, q2, q3), (s0, s1, s2, s3)
    s = scores(0, q0, s0)
    for k in range(KVH):
        following = scores(k + 1, q_refs[k + 1], kv_refs[k + 1]) if k + 1 < KVH else None
        finish(k, s)
        s = following


def combine_kernel(c0, c1, c2, c3, o0, o1, o2, o3):
    parts = (c0, c1, c2, c3)
    weights = []
    for k, out in enumerate((o0, o1, o2, o3)):
        group, lse = weigh([unpack_flat(ref[k, pl.ds(ROWS, 16), :]) for ref in parts])
        weights.append(group)
        out[pl.ds(ROWS, 16), :] = pack_flat(lse)
    outs = [[ref[k, pl.ds(0, ROWS), :].astype(F32) for ref in parts] for k in range(SIDE)]
    for out, mixed in zip((o0, o1, o2, o3), mix_all(weights, outs)):
        out[pl.ds(0, ROWS), :] = mixed.astype(BF)


def final_kernel(meta_ref, r0, r1, r2, r3, own_ref, lse_ref, out_ref):
    refs = (r0, r1, r2, r3)
    weights = [
        weigh([unpack_flat(ref[pl.ds(ROWS, 16), :]), lse_ref[k, pl.ds(0, 2), :]])[0] for k, ref in enumerate(refs)
    ]
    outs = [[ref[pl.ds(0, ROWS), :].astype(F32), own_ref[k]] for k, ref in enumerate(refs)]
    for k, mixed in enumerate(mix_all(weights, outs)):
        head = turned(meta_ref, k)
        for t in range(3):
            out_ref[t, head] = mixed[t * 64 : (t + 1) * 64].astype(BF)


def cost(flops, size, exps=0):
    return pl.CostEstimate(flops=flops, bytes_accessed=size, transcendentals=exps)


def shaped(shape, dtype=BF):
    return jax.ShapeDtypeStruct(shape, dtype)


def whole(array):
    return pl.BlockSpec(array.shape, lambda *_: (0,) * array.ndim)


def body(queries, new_kv, suffix_kv, suffix_len, pool_kv, sys_kv, block_slot, block_list, prefix_blocks):
    prompts = lax.axis_size("prompt")
    me_p = lax.axis_index("prompt")
    me_c = lax.axis_index("comp")
    y, x = me_c // SIDE, me_c % SIDE
    core = me_p % 2
    even = core == 0
    a = jnp.where(even, x, y)

    def send(array, role, step):
        return lax.ppermute(array, AXES, ring_pairs(prompts, role, step % SIDE))

    def source(k):
        return jnp.where(even, y * SIDE + (x - k + SIDE) % SIDE, ((y - k + SIDE) % SIDE) * SIDE + x) * 8

    zero = jnp.int32(0)
    meta = jnp.stack([y, x, a, source(0), source(1), source(2), source(3), core, zero]).astype(jnp.int32)

    far_sys = lax.ppermute(sys_kv, AXES, prompt_pairs(prompts, 1))
    places = jnp.arange(128, dtype=jnp.int32)
    listed = jnp.where(places[None, :64] < prefix_blocks[:1, None], block_list[:1], -1)
    far_listed = lax.ppermute(listed, AXES, row_pairs(prompts, 2))

    def one_head(array, k):
        return lax.dynamic_slice_in_dim(array, ((a + k) % SIDE) * HD, HD, array.ndim - 1).reshape(-1, HD)

    pieces = [one_head(pool_kv, 0)] + [send(one_head(pool_kv, k), "a", k) for k in (1, 2, 3)]

    q_msgs = pl.pallas_call(
        query_kernel,
        in_specs=[SMEM, VMEM, VMEM, VMEM],
        out_specs=[VMEM] * 4,
        out_shape=[shaped((ROWS + 2 * SYS_PART, HD))] * 4,
        scratch_shapes=[pltpu.VMEM((ROWS, HD), F32), pltpu.VMEM((2 * SYS_PART, HD), F32)],
        compiler_params=PARAMS,
        cost_estimate=cost(0, 2**19),
        name="query_messages",
    )(meta, queries.transpose(1, 0, 2), sys_kv, far_sys)
    q_got = [q_msgs[0]] + [send(q_msgs[k], "a", k) for k in (1, 2, 3)]
    stage, sys_one = pl.pallas_call(
        stage_kernel,
        in_specs=[VMEM] * 4,
        out_specs=[VMEM] * 2,
        out_shape=[shaped((SIDE, ROWS, HD)), shaped((1, 2, BLK, HD))],
        compiler_params=PARAMS,
        cost_estimate=cost(0, 2**19),
        name="stage",
    )(*q_got)
    columns = [stage] + [send(stage, "b", j) for j in (1, 2, 3)]
    sys_two = jnp.concatenate([sys_one, lax.ppermute(sys_one, AXES, prompt_pairs(prompts, 2))])
    sys_far = lax.ppermute(sys_two, AXES, prompt_pairs(prompts, 4))

    at_slot = block_slot[0][:, None] == places
    mine_first = y < 2
    both = jnp.where(
        mine_first, jnp.concatenate([listed, far_listed], axis=1), jnp.concatenate([far_listed, listed], axis=1)
    )
    used = jnp.any(both[0][:, None] == places, axis=0)
    mark = jnp.where(used, 1, 0) + jnp.where(places >= 64, 2, 0)
    code = jnp.sum(jnp.where(at_slot, mark[:, None], 0), axis=0)

    new_heads = jnp.stack([one_head(new_kv, k) for k in range(KVH)])
    own_out, own_lse = pl.pallas_call(
        own_kernel,
        in_specs=[SMEM] + [VMEM] * 9,
        out_specs=[VMEM] * 2,
        out_shape=[shaped((KVH, ROWS, HD), F32), shaped((KVH, 8, HD), F32)],
        scratch_shapes=[
            pltpu.VMEM((ROWS, 1024 + BLK), F32),
            pltpu.VMEM((2, 2048 + 2 * BLK, HD), F32),
            pltpu.VMEM((2, 1024 + BLK, 2 * HD), BF),
        ],
        compiler_params=PARAMS,
        cost_estimate=cost(2**30, 2**22, 2**20),
        name="own_tokens",
    )(suffix_len, *q_msgs, *[one_head(suffix_kv, k) for k in range(KVH)], new_heads)
    code, own_lse = lax.optimization_barrier((code, own_lse))

    operands = [*columns, *pieces, sys_two, sys_far]
    parts = pl.pallas_call(
        main_kernel,
        grid_spec=pltpu.PrefetchScalarGridSpec(
            num_scalar_prefetch=2,
            grid=(SIDE,),
            in_specs=[whole(one) for one in operands],
            out_specs=[pl.BlockSpec((SIDE, MSG, HD), lambda *_: (0, 0, 0))] * SIDE,
            scratch_shapes=[
                pltpu.VMEM((2, ALL_TOK, HD), BF),
                pltpu.VMEM((2, ALL_TOK, 2 * HD), BF),
                pltpu.VMEM((2, 20, 8, HD), F32),
                pltpu.VMEM((SIDE, SIDE, ROWS, HD), BF),
                pltpu.VMEM((SIDE, MSG, HD), BF),
                pltpu.VMEM((2, 2048, HD), F32),
            ],
        ),
        out_shape=[shaped((SIDE, MSG, HD))] * SIDE,
        compiler_params=PARAMS,
        cost_estimate=cost(2**33, 2**22, 2**23),
        name="attend",
    )(meta, code, *operands)
    parts = [parts[0]] + [send(parts[j], "b", -j) for j in (1, 2, 3)]
    back = pl.pallas_call(
        combine_kernel,
        in_specs=[VMEM] * 4,
        out_specs=[VMEM] * 4,
        out_shape=[shaped((MSG, HD))] * 4,
        compiler_params=PARAMS,
        cost_estimate=cost(0, 2**20),
        name="combine",
    )(*parts)
    heads = [back[0]] + [send(back[k], "a", -k) for k in (1, 2, 3)]
    out = pl.pallas_call(
        final_kernel,
        in_specs=[SMEM] + [VMEM] * 6,
        out_specs=VMEM,
        out_shape=shaped((3, KVH, 64, HD)),
        compiler_params=PARAMS,
        name="final",
    )(meta, *heads, own_out, own_lse)
    return out.reshape(3, KVH, GQ, 4, HD).transpose(3, 0, 1, 2, 4).reshape(4, 3, QH * HD)


def solution(mesh):
    both = P(AXES)
    in_specs = (both,) * 6 + (P("prompt"), both, both)
    return jax.shard_map(body, mesh=mesh, in_specs=in_specs, out_specs=both, check_vma=False)
```

```python
import functools

import jax
import jax.numpy as jnp
from jax import lax
from jax.experimental import pallas as pl
from jax.experimental.pallas import tpu as pltpu
from jax.sharding import PartitionSpec as P

QH = 64
KVH = 4
HD = 128
GQ = QH // KVH
SIDE = 4
BLK = 128
ROWS = 192
MSG = ROWS + 16
SYS_PART = 32
POOL_TOK = 512
ALL_TOK = 5 * POOL_TOK
AXES = ("prompt", "comp")
FLOOR = -1e30
SCALE2 = HD**-0.5 * 1.4426950408889634
BF = jnp.bfloat16
F32 = jnp.float32
NT = (((1,), (1,)), ((), ()))
PARAMS = pltpu.CompilerParams(vmem_limit_bytes=56 * 2**20)
SMEM = pl.BlockSpec(memory_space=pltpu.SMEM)
VMEM = pl.BlockSpec(memory_space=pltpu.VMEM)


def ring_pairs(prompts, role, step):
    pairs = []
    for p in range(prompts):
        along_x = (p % 2 == 0) == (role == "a")
        for y in range(SIDE):
            for x in range(SIDE):
                ty = y if along_x else (y + step) % SIDE
                tx = (x + step) % SIDE if along_x else x
                base = p * SIDE * SIDE
                pairs.append((base + y * SIDE + x, base + ty * SIDE + tx))
    return pairs


def ring_groups(prompts, role):
    step = ring_pairs(prompts, role, 1)
    follow = dict(step)
    groups = []
    for p in range(prompts):
        along_x = (p % 2 == 0) == (role == "a")
        for n in range(SIDE):
            group = [p * SIDE * SIDE + (n * SIDE if along_x else n)]
            while len(group) < SIDE:
                group.append(follow[group[-1]])
            groups.append(group)
    return groups


def row_pairs(prompts, step):
    count = SIDE * SIDE
    return [(p * count + c, p * count + (c + step * SIDE) % count) for p in range(prompts) for c in range(count)]


def prompt_pairs(prompts, bit):
    count = SIDE * SIDE
    return [(p * count + c, (p ^ bit) * count + c) for p in range(prompts) for c in range(count)]


def turned(meta_ref, k):
    return lax.rem(meta_ref[2] + k, SIDE)


def query_kernel(meta_ref, q_ref, sys_ref, far_ref, o0, o1, o2, o3, tmp, sys_tmp):
    for k, out in enumerate((o0, o1, o2, o3)):
        head = turned(meta_ref, k)
        for t in range(3):
            for g in range(GQ):
                at = pl.ds(pl.multiple_of((head * GQ + g) * HD, HD), HD)
                tmp[pl.ds(t * 64 + g * 4, 4), :] = q_ref[t, :, at].astype(F32)
        out[pl.ds(0, ROWS), :] = tmp[...].astype(BF)
        lanes = pl.ds(pl.multiple_of(head * HD, HD), HD)
        sys_tmp[pl.ds(0, SYS_PART), :] = sys_ref[:, :, lanes].reshape(SYS_PART, HD).astype(F32)
        sys_tmp[pl.ds(SYS_PART, SYS_PART), :] = far_ref[:, :, lanes].reshape(SYS_PART, HD).astype(F32)
        out[pl.ds(ROWS, SYS_PART), :] = sys_tmp[pl.ds(0, SYS_PART, stride=2), :].astype(BF)
        out[pl.ds(ROWS + SYS_PART, SYS_PART), :] = sys_tmp[pl.ds(1, SYS_PART, stride=2), :].astype(BF)


def stage_kernel(meta_ref, m0, m1, m2, m3, stage_ref, sys_ref):
    for k, msg in enumerate((m0, m1, m2, m3)):
        stage_ref[turned(meta_ref, SIDE - k)] = msg[pl.ds(0, ROWS), :]
        for side in range(2):
            at = pl.ds(k * SYS_PART, SYS_PART)
            sys_ref[0, side, at, :] = msg[pl.ds(ROWS + side * SYS_PART, SYS_PART), :]


def flatten_rows(lse):
    lane = lax.broadcasted_iota(jnp.int32, (BLK, HD), 1)
    row = lax.broadcasted_iota(jnp.int32, (BLK, HD), 0)
    rest = ROWS - BLK
    upper = jnp.sum(jnp.where(lane == row, lse[:BLK], 0.0), axis=0, keepdims=True)
    lower = jnp.sum(jnp.where((lane == row)[:rest], lse[BLK:], 0.0), axis=0, keepdims=True)
    return jnp.concatenate([upper, lower], axis=0)


def pack_flat(flat):
    hi = flat.astype(BF).astype(F32)
    mid = (flat - hi).astype(BF).astype(F32)
    low = flat - hi - mid
    return jnp.concatenate([hi, mid, low, jnp.zeros((10, HD), F32)], axis=0).astype(BF)


def unpack_flat(packed):
    wide = packed.astype(F32)
    return wide[0:2] + wide[2:4] + wide[4:6]


def weigh(flats):
    top = functools.reduce(jnp.maximum, flats)
    weights = [jnp.exp2(one - top) for one in flats]
    total = functools.reduce(jnp.add, weights)
    return [w / total for w in weights], top + jnp.log2(total)


def mix_all(weights, outs):
    flat = [w for group in weights for w in group]
    rows = 2 * len(flat)
    stacked = jnp.concatenate(flat + [jnp.zeros((HD - rows, HD), F32)], axis=0)
    columns = stacked.T
    mixed = []
    n = 0
    for group in outs:
        upper = lower = 0.0
        for one in group:
            upper = upper + columns[:, n : n + 1] * one[:BLK]
            lower = lower + columns[: ROWS - BLK, n + 1 : n + 2] * one[BLK:]
            n += 2
        mixed.append(jnp.concatenate([upper, lower], axis=0))
    return mixed


def main_kernel(cols, meta_ref, code_ref, *refs):
    count = len(cols)
    q_refs, pool_ref, sys_refs, refs = refs[:count], refs[count], refs[count + 1 : count + 3], refs[count + 3 :]
    o_refs, (kc, vc, bias, tmp) = refs[:count], refs[count:]
    pair = 2 * ROWS

    def fill():
        for p in range(2):
            vc[p, :, pl.ds(HD, HD)] = jnp.ones((ALL_TOK, HD), BF)
            for n in range(4):
                at = pl.ds(4 * POOL_TOK + n * BLK, BLK)
                kc[p, at, :] = sys_refs[n // 2][n % 2, 0]
                vc[p, at, pl.ds(0, HD)] = sys_refs[n // 2][n % 2, 1]
                bias[p, 16 + n] = jnp.zeros((8, HD), F32)
        for k in range(SIDE):
            held = tmp.at[k % 2]
            held[...] = pool_ref[k].astype(F32)
            n0, n1 = jnp.int32(0), jnp.int32(0)
            for blk in range(8):
                code = code_ref[meta_ref[3 + k] + blk]
                prompt = code // 2
                rank = k * 4 + jnp.minimum(jnp.where(prompt == 0, n0, n1), 3)
                at = pl.ds(pl.multiple_of(rank * BLK, BLK), BLK)
                kc[prompt, at, :] = held[pl.ds(blk * 2 * BLK, BLK, stride=2), :].astype(BF)
                vc[prompt, at, pl.ds(0, HD)] = held[pl.ds(blk * 2 * BLK + 1, BLK, stride=2), :].astype(BF)
                dead = jnp.where(code % 2 == 1, 0.0, FLOOR)
                bias[prompt, rank] = jnp.full((8, HD), dead, F32)
                n0 = n0 + 1 - prompt
                n1 = n1 + prompt

    def prompt_of(i, n):
        row = lax.rem(meta_ref[0] - cols[i] + SIDE, SIDE)
        return jnp.where(meta_ref[7] == 0, row // 2, n)

    def scores(i, n):
        p = prompt_of(i, n)
        q = q_refs[i][2 * n : 2 * n + 2].reshape(pair, HD)
        s = lax.dot_general(q, kc[p], NT, preferred_element_type=F32)
        return s + jnp.concatenate([bias[p, t, :1, :] for t in range(20)], axis=1)

    def finish(i, n, s):
        m = jnp.max(s, axis=1, keepdims=True)
        w = jnp.exp2((s - m) * SCALE2).astype(BF)
        acc = jnp.dot(w, vc[prompt_of(i, n)], preferred_element_type=F32)
        total = acc[:, HD:]
        out = (acc[:, :HD] / total).astype(BF)
        lse = m * SCALE2 + jnp.log2(total)
        for half in range(2):
            part = slice(half * ROWS, (half + 1) * ROWS)
            o_refs[i][2 * n + half, pl.ds(0, ROWS), :] = out[part]
            o_refs[i][2 * n + half, pl.ds(ROWS, 16), :] = pack_flat(flatten_rows(lse[part]))

    fill()
    jobs = [(i, n) for i in range(count) for n in range(2)]
    s = scores(*jobs[0])
    for t, job in enumerate(jobs):
        following = scores(*jobs[t + 1]) if t + 1 < len(jobs) else None
        finish(*job, s)
        s = following


def own_kernel(lens_ref, q0, q1, q2, q3, s0, s1, s2, s3, new_ref, o_ref, lse_ref, bias, tmp, vc):
    tokens = vc.shape[1]
    comp = lax.broadcasted_iota(jnp.int32, (ROWS, 256), 0) % 4
    place = lax.broadcasted_iota(jnp.int32, (ROWS, 256), 1)
    for c in range(4):
        live = (comp == c) & (place < lens_ref[c])
        bias[:, pl.ds(c * 256, 256)] = jnp.where(live, 0.0, FLOOR)
    row = lax.broadcasted_iota(jnp.int32, (ROWS, BLK), 0)
    col = lax.broadcasted_iota(jnp.int32, (ROWS, BLK), 1)
    fresh = col - (row % 4) * 3
    bias[:, pl.ds(1024, BLK)] = jnp.where((fresh >= 0) & (fresh < 3) & (fresh <= row // 64), 0.0, FLOOR)
    for n in range(2):
        vc[n, :, pl.ds(HD, HD)] = jnp.ones((tokens, HD), BF)
        tmp[n, pl.ds(2048, 256), :] = jnp.zeros((256, HD), F32)

    def scores(k, q_ref, kv_ref):
        held = tmp.at[k % 2]
        held[pl.ds(0, 2048), :] = kv_ref[...].astype(F32)
        held[pl.ds(2048, 24), :] = new_ref[k].astype(F32)
        key = held[pl.ds(0, tokens, stride=2), :].astype(BF)
        vc[k % 2, :, pl.ds(0, HD)] = held[pl.ds(1, tokens, stride=2), :].astype(BF)
        s = lax.dot_general(q_ref[pl.ds(0, ROWS), :], key, NT, preferred_element_type=F32)
        return s + bias[...]

    def finish(k, s):
        m = jnp.max(s, axis=1, keepdims=True)
        w = jnp.exp2((s - m) * SCALE2).astype(BF)
        acc = jnp.dot(w, vc[k % 2], preferred_element_type=F32)
        total = acc[:, HD:]
        o_ref[k] = acc[:, :HD] / total
        lse_ref[k, pl.ds(0, 2), :] = flatten_rows(m * SCALE2 + jnp.log2(total))

    q_refs, kv_refs = (q0, q1, q2, q3), (s0, s1, s2, s3)
    s = scores(0, q0, s0)
    for k in range(KVH):
        following = scores(k + 1, q_refs[k + 1], kv_refs[k + 1]) if k + 1 < KVH else None
        finish(k, s)
        s = following


def combine_kernel(meta_ref, c0, c1, c2, c3, o0, o1, o2, o3):
    parts = (c0, c1, c2, c3)
    weights, outs = [], []
    for k, out in enumerate((o0, o1, o2, o3)):
        n = turned(meta_ref, SIDE - k)
        group, lse = weigh([unpack_flat(ref[n, pl.ds(ROWS, 16), :]) for ref in parts])
        weights.append(group)
        outs.append([ref[n, pl.ds(0, ROWS), :].astype(F32) for ref in parts])
        out[pl.ds(ROWS, 16), :] = pack_flat(lse)
    for out, mixed in zip((o0, o1, o2, o3), mix_all(weights, outs)):
        out[pl.ds(0, ROWS), :] = mixed.astype(BF)


def final_kernel(meta_ref, r0, r1, r2, r3, own_ref, lse_ref, out_ref):
    refs = (r0, r1, r2, r3)
    weights = [
        weigh([unpack_flat(ref[pl.ds(ROWS, 16), :]), lse_ref[k, pl.ds(0, 2), :]])[0] for k, ref in enumerate(refs)
    ]
    outs = [[ref[pl.ds(0, ROWS), :].astype(F32), own_ref[k]] for k, ref in enumerate(refs)]
    for k, mixed in enumerate(mix_all(weights, outs)):
        head = turned(meta_ref, k)
        for t in range(3):
            out_ref[t, head] = mixed[t * 64 : (t + 1) * 64].astype(BF)


def cost(flops, size, exps=0):
    return pl.CostEstimate(flops=flops, bytes_accessed=size, transcendentals=exps)


def shaped(shape, dtype=BF):
    return jax.ShapeDtypeStruct(shape, dtype)


def whole(array):
    return pl.BlockSpec(array.shape, lambda *_: (0,) * array.ndim)


def body(queries, new_kv, suffix_kv, suffix_len, pool_kv, sys_kv, block_slot, block_list, prefix_blocks):
    prompts = lax.axis_size("prompt")
    me_p = lax.axis_index("prompt")
    me_c = lax.axis_index("comp")
    y, x = me_c // SIDE, me_c % SIDE
    core = me_p % 2
    even = core == 0
    a = jnp.where(even, x, y)

    def send(array, role, step):
        return lax.ppermute(array, AXES, ring_pairs(prompts, role, step % SIDE))

    def source(n):
        return jnp.where(even, y * SIDE + n, n * SIDE + x) * 8

    zero = jnp.int32(0)
    meta = jnp.stack([y, x, a, source(0), source(1), source(2), source(3), core, zero]).astype(jnp.int32)

    far_sys = lax.ppermute(sys_kv, AXES, prompt_pairs(prompts, 1))
    def one_head(array, k):
        return lax.dynamic_slice_in_dim(array, ((a + k) % SIDE) * HD, HD, array.ndim - 1).reshape(-1, HD)

    by_head = jnp.stack([pool_kv[..., h * HD : (h + 1) * HD].reshape(-1, HD) for h in range(KVH)])

    q_msgs = pl.pallas_call(
        query_kernel,
        in_specs=[SMEM, VMEM, VMEM, VMEM],
        out_specs=[VMEM] * 4,
        out_shape=[shaped((ROWS + 2 * SYS_PART, HD))] * 4,
        scratch_shapes=[pltpu.VMEM((ROWS, HD), F32), pltpu.VMEM((2 * SYS_PART, HD), F32)],
        compiler_params=PARAMS,
        cost_estimate=cost(0, 2**19),
        name="query_messages",
    )(meta, queries.transpose(1, 0, 2), sys_kv, far_sys)
    q_msgs = list(q_msgs)
    places = jnp.arange(128, dtype=jnp.int32)
    block_list, q_msgs[0] = lax.optimization_barrier((block_list, q_msgs[0]))
    listed = jnp.where(places[None, :64] < prefix_blocks[:1, None], block_list[:1], -1)
    far_listed = lax.ppermute(listed, AXES, row_pairs(prompts, 2))
    q_got = [q_msgs[0]] + [send(q_msgs[k], "a", k) for k in (1, 2, 3)]
    by_head, *q_got = lax.optimization_barrier((by_head, *q_got))
    pool = lax.all_to_all(by_head, AXES, 0, 0, axis_index_groups=ring_groups(prompts, "a"), tiled=True)
    stage, sys_one = pl.pallas_call(
        stage_kernel,
        in_specs=[SMEM] + [VMEM] * 4,
        out_specs=[VMEM] * 2,
        out_shape=[shaped((SIDE, ROWS, HD)), shaped((1, 2, BLK, HD))],
        compiler_params=PARAMS,
        cost_estimate=cost(0, 2**19),
        name="stage",
    )(meta, *q_got)
    columns = [stage] + [send(stage, "b", j) for j in (1, 2, 3)]
    sys_two = jnp.concatenate([sys_one, lax.ppermute(sys_one, AXES, prompt_pairs(prompts, 2))])
    sys_far = lax.ppermute(sys_two, AXES, prompt_pairs(prompts, 4))

    at_slot = block_slot[0][:, None] == places
    far_listed, *columns = lax.optimization_barrier((far_listed, *columns))
    mine_first = y < 2
    both = jnp.where(
        mine_first, jnp.concatenate([listed, far_listed], axis=1), jnp.concatenate([far_listed, listed], axis=1)
    )
    used = jnp.any(both[0][:, None] == places, axis=0)
    mark = jnp.where(used, 1, 0) + jnp.where(places >= 64, 2, 0)
    code = jnp.sum(jnp.where(at_slot, mark[:, None], 0), axis=0)

    def attend(cols):
        operands = [columns[j] for j in cols] + [pool, sys_two, sys_far]
        return pl.pallas_call(
            functools.partial(main_kernel, cols),
            grid_spec=pltpu.PrefetchScalarGridSpec(
                num_scalar_prefetch=2,
                grid=(1,),
                in_specs=[whole(one) for one in operands],
                out_specs=[pl.BlockSpec((SIDE, MSG, HD), lambda *_: (0, 0, 0))] * len(cols),
                scratch_shapes=[
                    pltpu.VMEM((2, ALL_TOK, HD), BF),
                    pltpu.VMEM((2, ALL_TOK, 2 * HD), BF),
                    pltpu.VMEM((2, 20, 8, HD), F32),
                    pltpu.VMEM((2, 2048, HD), F32),
                ],
            ),
            out_shape=[shaped((SIDE, MSG, HD))] * len(cols),
            compiler_params=PARAMS,
            cost_estimate=cost(len(cols) * 2**31, 2**22, len(cols) * 2**21),
            name="attend_%d" % len(cols),
        )(meta, code, *operands)

    parts = list(attend((0, 1, 2, 3)))
    parts = [parts[0]] + [send(parts[j], "b", -j) for j in (1, 2, 3)]
    suffix_len, suffix_kv, parts[0] = lax.optimization_barrier((suffix_len, suffix_kv, parts[0]))
    new_heads = jnp.stack([one_head(new_kv, k) for k in range(KVH)])
    own_out, own_lse = pl.pallas_call(
        own_kernel,
        in_specs=[SMEM] + [VMEM] * 9,
        out_specs=[VMEM] * 2,
        out_shape=[shaped((KVH, ROWS, HD), F32), shaped((KVH, 8, HD), F32)],
        scratch_shapes=[
            pltpu.VMEM((ROWS, 1024 + BLK), F32),
            pltpu.VMEM((2, 2048 + 2 * BLK, HD), F32),
            pltpu.VMEM((2, 1024 + BLK, 2 * HD), BF),
        ],
        compiler_params=PARAMS,
        cost_estimate=cost(2**30, 2**22, 2**20),
        name="own_tokens",
    )(suffix_len, *q_msgs, *[one_head(suffix_kv, k) for k in range(KVH)], new_heads)
    back = pl.pallas_call(
        combine_kernel,
        in_specs=[SMEM] + [VMEM] * 4,
        out_specs=[VMEM] * 4,
        out_shape=[shaped((MSG, HD))] * 4,
        compiler_params=PARAMS,
        cost_estimate=cost(0, 2**20),
        name="combine",
    )(meta, *parts)
    heads = [back[0]] + [send(back[k], "a", -k) for k in (1, 2, 3)]
    out = pl.pallas_call(
        final_kernel,
        in_specs=[SMEM] + [VMEM] * 6,
        out_specs=VMEM,
        out_shape=shaped((3, KVH, 64, HD)),
        compiler_params=PARAMS,
        name="final",
    )(meta, *heads, own_out, own_lse)
    return out.reshape(3, KVH, GQ, 4, HD).transpose(3, 0, 1, 2, 4).reshape(4, 3, QH * HD)


def solution(mesh):
    both = P(AXES)
    in_specs = (both,) * 6 + (P("prompt"), both, both)
    return jax.shard_map(body, mesh=mesh, in_specs=in_specs, out_specs=both, check_vma=False)
```

```python
import functools

import jax
import jax.numpy as jnp
from jax import lax
from jax.experimental import pallas as pl
from jax.experimental.pallas import tpu as pltpu
from jax.sharding import PartitionSpec as P

QH = 64
KVH = 4
HD = 128
GQ = QH // KVH
SIDE = 4
BLK = 128
ROWS = 192
MSG = ROWS + 16
SYS_PART = 32
POOL_TOK = 512
ALL_TOK = 5 * POOL_TOK
AXES = ("prompt", "comp")
FLOOR = -1e30
SCALE2 = HD**-0.5 * 1.4426950408889634
BF = jnp.bfloat16
F32 = jnp.float32
NT = (((1,), (1,)), ((), ()))


def room(mib):
    return pltpu.CompilerParams(vmem_limit_bytes=mib * 2**20)


SMEM = pl.BlockSpec(memory_space=pltpu.SMEM)
VMEM = pl.BlockSpec(memory_space=pltpu.VMEM)


def ring_pairs(prompts, role, step):
    pairs = []
    for p in range(prompts):
        along_x = (p % 2 == 0) == (role == "a")
        for y in range(SIDE):
            for x in range(SIDE):
                ty = y if along_x else (y + step) % SIDE
                tx = (x + step) % SIDE if along_x else x
                base = p * SIDE * SIDE
                pairs.append((base + y * SIDE + x, base + ty * SIDE + tx))
    return pairs


def ring_groups(prompts, role):
    step = ring_pairs(prompts, role, 1)
    follow = dict(step)
    groups = []
    for p in range(prompts):
        along_x = (p % 2 == 0) == (role == "a")
        for n in range(SIDE):
            group = [p * SIDE * SIDE + (n * SIDE if along_x else n)]
            while len(group) < SIDE:
                group.append(follow[group[-1]])
            groups.append(group)
    return groups


def core_pairs(prompts):
    count = SIDE * SIDE
    return [(p * count + c, (p ^ 1) * count + c) for p in range(prompts) for c in range(count)]


def plane_pairs(prompts, step):
    count = SIDE * SIDE
    return [(p * count + c, (p + 2 * step) % prompts * count + c) for p in range(prompts) for c in range(count)]


def turned(meta_ref, k):
    return lax.rem(meta_ref[2] + k, SIDE)


def query_kernel(meta_ref, slot_ref, list_ref, used_ref, q_ref, sys_ref, far_ref, o0, o1, o2, o3, tmp, sys_tmp):
    lane = lax.broadcasted_iota(jnp.int32, (16, HD), 1)
    flags = jnp.zeros((16, HD), F32)
    for n in range(64):
        slot = jnp.where(n < used_ref[0], slot_ref[0, list_ref[0, n]], -1)
        flags = jnp.where(lane == slot, 1.0, flags)
    for k, out in enumerate((o0, o1, o2, o3)):
        head = turned(meta_ref, k)
        for t in range(3):
            for g in range(GQ):
                at = pl.ds(pl.multiple_of((head * GQ + g) * HD, HD), HD)
                tmp[pl.ds(t * 64 + g * 4, 4), :] = q_ref[t, :, at].astype(F32)
        out[pl.ds(0, ROWS), :] = tmp[...].astype(BF)
        lanes = pl.ds(pl.multiple_of(head * HD, HD), HD)
        sys_tmp[pl.ds(0, SYS_PART), :] = sys_ref[:, :, lanes].reshape(SYS_PART, HD).astype(F32)
        sys_tmp[pl.ds(SYS_PART, SYS_PART), :] = far_ref[:, :, lanes].reshape(SYS_PART, HD).astype(F32)
        out[pl.ds(MSG, SYS_PART), :] = sys_tmp[pl.ds(0, SYS_PART, stride=2), :].astype(BF)
        out[pl.ds(MSG + SYS_PART, SYS_PART), :] = sys_tmp[pl.ds(1, SYS_PART, stride=2), :].astype(BF)
        out[pl.ds(ROWS, 16), :] = flags.astype(BF)


def stage_kernel(meta_ref, m0, m1, m2, m3, stage_ref, sys_ref):
    for k, msg in enumerate((m0, m1, m2, m3)):
        stage_ref[turned(meta_ref, SIDE - k)] = msg[pl.ds(0, MSG), :]
        for side in range(2):
            at = pl.ds(k * SYS_PART, SYS_PART)
            sys_ref[side, at, :] = msg[pl.ds(MSG + side * SYS_PART, SYS_PART), :]


def flatten_rows(lse):
    lane = lax.broadcasted_iota(jnp.int32, (BLK, HD), 1)
    row = lax.broadcasted_iota(jnp.int32, (BLK, HD), 0)
    rest = ROWS - BLK
    upper = jnp.sum(jnp.where(lane == row, lse[:BLK], 0.0), axis=0, keepdims=True)
    lower = jnp.sum(jnp.where((lane == row)[:rest], lse[BLK:], 0.0), axis=0, keepdims=True)
    return jnp.concatenate([upper, lower], axis=0)


def pack_flat(flat):
    hi = flat.astype(BF).astype(F32)
    mid = (flat - hi).astype(BF).astype(F32)
    low = flat - hi - mid
    return jnp.concatenate([hi, mid, low, jnp.zeros((10, HD), F32)], axis=0).astype(BF)


def unpack_flat(packed):
    wide = packed.astype(F32)
    return wide[0:2] + wide[2:4] + wide[4:6]


def weigh(flats):
    top = functools.reduce(jnp.maximum, flats)
    weights = [jnp.exp2(one - top) for one in flats]
    total = functools.reduce(jnp.add, weights)
    return [w / total for w in weights], top + jnp.log2(total)


def mix_all(weights, outs):
    flat = [w for group in weights for w in group]
    rows = 2 * len(flat)
    stacked = jnp.concatenate(flat + [jnp.zeros((HD - rows, HD), F32)], axis=0)
    columns = stacked.T
    mixed = []
    n = 0
    for group in outs:
        upper = lower = 0.0
        for one in group:
            upper = upper + columns[:, n : n + 1] * one[:BLK]
            lower = lower + columns[: ROWS - BLK, n + 1 : n + 2] * one[BLK:]
            n += 2
        mixed.append(jnp.concatenate([upper, lower], axis=0))
    return mixed


def main_kernel(meta_ref, owner_ref, *refs):
    q_refs, pool_ref, sys_refs, o_refs, refs = refs[:4], refs[4], refs[5:9], refs[9:13], refs[13:]
    kc, vc, bias, tmp, raw, sems = refs
    pair = 2 * ROWS
    copies = [pltpu.make_async_copy(pool_ref.at[k], raw.at[k], sems.at[k]) for k in range(SIDE)]
    for copy in copies:
        copy.start()

    def used_slots(prompt):
        column = lax.rem(meta_ref[0] - 2 * prompt + SIDE, SIDE)
        row = pl.ds(ROWS, 1)
        flags = q_refs[0][2 * prompt, row, :].astype(F32)
        for j in range(SIDE):
            chosen = (meta_ref[7] == 0) & (column == j)
            flags = jnp.where(chosen, q_refs[j][0, row, :].astype(F32), flags)
        return flags

    flags = [used_slots(0), used_slots(1)]
    lane = lax.broadcasted_iota(jnp.int32, (1, HD), 1)
    for p in range(2):
        vc[p, :, pl.ds(HD, HD)] = jnp.ones((ALL_TOK, HD), BF)
        for n in range(4):
            at = pl.ds(4 * POOL_TOK + n * BLK, BLK)
            kc[p, at, :] = sys_refs[n][0]
            vc[p, at, pl.ds(0, HD)] = sys_refs[n][1]
            bias[p, 16 + n] = jnp.zeros((8, HD), F32)
    for k in range(SIDE):
        copies[k].wait()
        held = tmp.at[k % 2]
        held[...] = raw[k].astype(F32)
        n0, n1 = jnp.int32(0), jnp.int32(0)
        for blk in range(8):
            slot = meta_ref[3 + k] + blk
            prompt = owner_ref[slot]
            rank = k * 4 + jnp.minimum(jnp.where(prompt == 0, n0, n1), 3)
            at = pl.ds(pl.multiple_of(rank * BLK, BLK), BLK)
            kc[prompt, at, :] = held[pl.ds(blk * 2 * BLK, BLK, stride=2), :].astype(BF)
            vc[prompt, at, pl.ds(0, HD)] = held[pl.ds(blk * 2 * BLK + 1, BLK, stride=2), :].astype(BF)
            live = jnp.where(prompt == 0, flags[0], flags[1])
            live = jnp.sum(jnp.where(lane == slot, live, 0.0), axis=1, keepdims=True)
            bias[prompt, rank] = jnp.broadcast_to((1.0 - live) * FLOOR, (8, HD))
            n0 = n0 + 1 - prompt
            n1 = n1 + prompt

    def prompt_of(i, n):
        row = lax.rem(meta_ref[0] - i + SIDE, SIDE)
        return jnp.where(meta_ref[7] == 0, row // 2, n)

    def scores(i, n):
        p = prompt_of(i, n)
        q = q_refs[i][2 * n : 2 * n + 2, :ROWS].reshape(pair, HD)
        s = lax.dot_general(q, kc[p], NT, preferred_element_type=F32)
        return s + jnp.concatenate([bias[p, t, :1, :] for t in range(20)], axis=1)

    def finish(i, n, s):
        m = jnp.max(s, axis=1, keepdims=True)
        w = jnp.exp2((s - m) * SCALE2).astype(BF)
        acc = jnp.dot(w, vc[prompt_of(i, n)], preferred_element_type=F32)
        total = acc[:, HD:]
        out = (acc[:, :HD] / total).astype(BF)
        lse = m * SCALE2 + jnp.log2(total)
        for half in range(2):
            part = slice(half * ROWS, (half + 1) * ROWS)
            o_refs[i][2 * n + half, pl.ds(0, ROWS), :] = out[part]
            o_refs[i][2 * n + half, pl.ds(ROWS, 16), :] = pack_flat(flatten_rows(lse[part]))

    jobs = [(i, n) for i in range(SIDE) for n in range(2)]
    s = scores(*jobs[0])
    for t, job in enumerate(jobs):
        following = scores(*jobs[t + 1]) if t + 1 < len(jobs) else None
        finish(*job, s)
        s = following


def own_kernel(lens_ref, q0, q1, q2, q3, s0, s1, s2, s3, new_ref, o_ref, lse_ref, bias, tmp, vc):
    tokens = vc.shape[1]
    comp = lax.broadcasted_iota(jnp.int32, (ROWS, 256), 0) % 4
    place = lax.broadcasted_iota(jnp.int32, (ROWS, 256), 1)
    for c in range(4):
        live = (comp == c) & (place < lens_ref[c])
        bias[:, pl.ds(c * 256, 256)] = jnp.where(live, 0.0, FLOOR)
    row = lax.broadcasted_iota(jnp.int32, (ROWS, BLK), 0)
    col = lax.broadcasted_iota(jnp.int32, (ROWS, BLK), 1)
    fresh = col - (row % 4) * 3
    bias[:, pl.ds(1024, BLK)] = jnp.where((fresh >= 0) & (fresh < 3) & (fresh <= row // 64), 0.0, FLOOR)
    for n in range(2):
        vc[n, :, pl.ds(HD, HD)] = jnp.ones((tokens, HD), BF)
        tmp[n, pl.ds(2048, 256), :] = jnp.zeros((256, HD), F32)

    def scores(k, q_ref, kv_ref):
        held = tmp.at[k % 2]
        held[pl.ds(0, 2048), :] = kv_ref[...].astype(F32)
        held[pl.ds(2048, 24), :] = new_ref[k].astype(F32)
        key = held[pl.ds(0, tokens, stride=2), :].astype(BF)
        vc[k % 2, :, pl.ds(0, HD)] = held[pl.ds(1, tokens, stride=2), :].astype(BF)
        s = lax.dot_general(q_ref[pl.ds(0, ROWS), :], key, NT, preferred_element_type=F32)
        return s + bias[...]

    def finish(k, s):
        m = jnp.max(s, axis=1, keepdims=True)
        w = jnp.exp2((s - m) * SCALE2).astype(BF)
        acc = jnp.dot(w, vc[k % 2], preferred_element_type=F32)
        total = acc[:, HD:]
        o_ref[k] = acc[:, :HD] / total
        lse_ref[k, pl.ds(0, 2), :] = flatten_rows(m * SCALE2 + jnp.log2(total))

    q_refs, kv_refs = (q0, q1, q2, q3), (s0, s1, s2, s3)
    s = scores(0, q0, s0)
    for k in range(KVH):
        following = scores(k + 1, q_refs[k + 1], kv_refs[k + 1]) if k + 1 < KVH else None
        finish(k, s)
        s = following


def combine_kernel(meta_ref, c0, c1, c2, c3, o0, o1, o2, o3):
    parts = (c0, c1, c2, c3)
    weights, outs = [], []
    for k, out in enumerate((o0, o1, o2, o3)):
        n = turned(meta_ref, SIDE - k)
        group, lse = weigh([unpack_flat(ref[n, pl.ds(ROWS, 16), :]) for ref in parts])
        weights.append(group)
        outs.append([ref[n, pl.ds(0, ROWS), :].astype(F32) for ref in parts])
        out[pl.ds(ROWS, 16), :] = pack_flat(lse)
    for out, mixed in zip((o0, o1, o2, o3), mix_all(weights, outs)):
        out[pl.ds(0, ROWS), :] = mixed.astype(BF)


def final_kernel(meta_ref, r0, r1, r2, r3, own_ref, lse_ref, out_ref):
    refs = (r0, r1, r2, r3)
    weights = [
        weigh([unpack_flat(ref[pl.ds(ROWS, 16), :]), lse_ref[k, pl.ds(0, 2), :]])[0] for k, ref in enumerate(refs)
    ]
    outs = [[ref[pl.ds(0, ROWS), :].astype(F32), own_ref[k]] for k, ref in enumerate(refs)]
    for k, mixed in enumerate(mix_all(weights, outs)):
        head = turned(meta_ref, k)
        for t in range(3):
            out_ref[t, head] = mixed[t * 64 : (t + 1) * 64].astype(BF)


def cost(flops, size, exps=0):
    return pl.CostEstimate(flops=flops, bytes_accessed=size, transcendentals=exps)


def shaped(shape, dtype=BF):
    return jax.ShapeDtypeStruct(shape, dtype)


def whole(array):
    return pl.BlockSpec(array.shape, lambda *_: (0,) * array.ndim)


def body(queries, new_kv, suffix_kv, suffix_len, pool_kv, sys_kv, block_slot, block_list, prefix_blocks):
    prompts = lax.axis_size("prompt")
    me_p = lax.axis_index("prompt")
    me_c = lax.axis_index("comp")
    y, x = me_c // SIDE, me_c % SIDE
    core = me_p % 2
    even = core == 0
    a = jnp.where(even, x, y)

    def send(array, role, step):
        return lax.ppermute(array, AXES, ring_pairs(prompts, role, step % SIDE))

    def source(n):
        return jnp.where(even, y * SIDE + n, n * SIDE + x) * 8

    meta = jnp.stack([y, x, a, source(0), source(1), source(2), source(3), core]).astype(jnp.int32)

    far_sys = lax.ppermute(sys_kv, AXES, core_pairs(prompts))

    def one_head(array, k):
        return lax.dynamic_slice_in_dim(array, ((a + k) % SIDE) * HD, HD, array.ndim - 1).reshape(-1, HD)

    by_head = jnp.stack([pool_kv[..., h * HD : (h + 1) * HD].reshape(-1, HD) for h in range(KVH)])

    q_msgs = pl.pallas_call(
        query_kernel,
        in_specs=[SMEM] * 4 + [VMEM] * 3,
        out_specs=[VMEM] * 4,
        out_shape=[shaped((MSG + 2 * SYS_PART, HD))] * 4,
        scratch_shapes=[pltpu.VMEM((ROWS, HD), F32), pltpu.VMEM((2 * SYS_PART, HD), F32)],
        compiler_params=room(10),
        cost_estimate=cost(0, 2**19),
        name="query_messages",
    )(meta, block_slot, block_list, prefix_blocks, queries.transpose(1, 0, 2), sys_kv, far_sys)
    q_got = [q_msgs[0]] + [send(q_msgs[k], "a", k) for k in (1, 2, 3)]
    by_head, *q_got = lax.optimization_barrier((by_head, *q_got))
    pool = lax.all_to_all(by_head, AXES, 0, 0, axis_index_groups=ring_groups(prompts, "a"), tiled=True)
    stage, sys_one = pl.pallas_call(
        stage_kernel,
        in_specs=[SMEM] + [VMEM] * 4,
        out_specs=[VMEM] * 2,
        out_shape=[shaped((SIDE, MSG, HD)), shaped((2, BLK, HD))],
        compiler_params=room(8),
        cost_estimate=cost(0, 2**19),
        name="stage",
    )(meta, *q_got)
    columns = [stage] + [send(stage, "b", j) for j in (1, 2, 3)]
    system = [sys_one] + [lax.ppermute(sys_one, AXES, plane_pairs(prompts, k)) for k in (1, 2, 3)]

    places = jnp.arange(128, dtype=jnp.int32)
    owner = jnp.sum(jnp.where((block_slot[0][:, None] == places) & (places[:, None] >= 64), 1, 0), axis=0)

    parts = pl.pallas_call(
        main_kernel,
        grid_spec=pltpu.PrefetchScalarGridSpec(
            num_scalar_prefetch=2,
            grid=(1,),
            in_specs=[whole(one) for one in columns] + [pl.BlockSpec(memory_space=pl.ANY)] + [whole(sys_one)] * 4,
            out_specs=[pl.BlockSpec((SIDE, MSG, HD), lambda *_: (0, 0, 0))] * SIDE,
            scratch_shapes=[
                pltpu.VMEM((2, ALL_TOK, HD), BF),
                pltpu.VMEM((2, ALL_TOK, 2 * HD), BF),
                pltpu.VMEM((2, 20, 8, HD), F32),
                pltpu.VMEM((2, 2048, HD), F32),
                pltpu.VMEM((SIDE, 2048, HD), BF),
                pltpu.SemaphoreType.DMA((SIDE,)),
            ],
        ),
        out_shape=[shaped((SIDE, MSG, HD))] * SIDE,
        compiler_params=room(38),
        cost_estimate=cost(2**33, 2**22, 2**23),
        name="attend",
    )(meta, owner, *columns, pool, *system)
    parts = list(parts)
    parts = [parts[0]] + [send(parts[j], "b", -j) for j in (1, 2, 3)]
    suffix_len, parts[0] = lax.optimization_barrier((suffix_len, parts[0]))
    new_heads = jnp.stack([one_head(new_kv, k) for k in range(KVH)])
    own_out, own_lse = pl.pallas_call(
        own_kernel,
        in_specs=[SMEM] + [VMEM] * 9,
        out_specs=[VMEM] * 2,
        out_shape=[shaped((KVH, ROWS, HD), F32), shaped((KVH, 8, HD), F32)],
        scratch_shapes=[
            pltpu.VMEM((ROWS, 1024 + BLK), F32),
            pltpu.VMEM((2, 2048 + 2 * BLK, HD), F32),
            pltpu.VMEM((2, 1024 + BLK, 2 * HD), BF),
        ],
        compiler_params=room(20),
        cost_estimate=cost(2**30, 2**22, 2**20),
        name="own_tokens",
    )(suffix_len, *q_msgs, *[one_head(suffix_kv, k) for k in range(KVH)], new_heads)
    back = pl.pallas_call(
        combine_kernel,
        in_specs=[SMEM] + [VMEM] * 4,
        out_specs=[VMEM] * 4,
        out_shape=[shaped((MSG, HD))] * 4,
        compiler_params=room(10),
        cost_estimate=cost(0, 2**20),
        name="combine",
    )(meta, *parts)
    heads = [back[0]] + [send(back[k], "a", -k) for k in (1, 2, 3)]
    out = pl.pallas_call(
        final_kernel,
        in_specs=[SMEM] + [VMEM] * 6,
        out_specs=VMEM,
        out_shape=shaped((3, KVH, 64, HD)),
        compiler_params=room(10),
        name="final",
    )(meta, *heads, own_out, own_lse)
    return out.reshape(3, KVH, GQ, 4, HD).transpose(3, 0, 1, 2, 4).reshape(4, 3, QH * HD)


def solution(mesh):
    both = P(AXES)
    in_specs = (both,) * 6 + (P("prompt"), both, both)
    return jax.shard_map(body, mesh=mesh, in_specs=in_specs, out_specs=both, check_vma=False)
```

```python
import functools

import jax
import jax.numpy as jnp
from jax import lax
from jax.experimental import pallas as pl
from jax.experimental.pallas import tpu as pltpu
from jax.sharding import PartitionSpec as P

QH = 64
KVH = 4
HD = 128
GQ = QH // KVH
SIDE = 4
BLK = 128
ROWS = 192
MSG = ROWS + 16
SYS_PART = 32
POOL_TOK = 512
ALL_TOK = 5 * POOL_TOK
AXES = ("prompt", "comp")
FLOOR = -1e30
SCALE2 = HD**-0.5 * 1.4426950408889634
BF = jnp.bfloat16
F32 = jnp.float32
NT = (((1,), (1,)), ((), ()))


def room(mib):
    return pltpu.CompilerParams(vmem_limit_bytes=mib * 2**20)


SMEM = pl.BlockSpec(memory_space=pltpu.SMEM)
VMEM = pl.BlockSpec(memory_space=pltpu.VMEM)


def ring_pairs(prompts, role, step):
    pairs = []
    for p in range(prompts):
        along_x = (p % 2 == 0) == (role == "a")
        for y in range(SIDE):
            for x in range(SIDE):
                ty = y if along_x else (y + step) % SIDE
                tx = (x + step) % SIDE if along_x else x
                base = p * SIDE * SIDE
                pairs.append((base + y * SIDE + x, base + ty * SIDE + tx))
    return pairs


def ring_groups(prompts, role):
    step = ring_pairs(prompts, role, 1)
    follow = dict(step)
    groups = []
    for p in range(prompts):
        along_x = (p % 2 == 0) == (role == "a")
        for n in range(SIDE):
            group = [p * SIDE * SIDE + (n * SIDE if along_x else n)]
            while len(group) < SIDE:
                group.append(follow[group[-1]])
            groups.append(group)
    return groups


def core_pairs(prompts):
    count = SIDE * SIDE
    return [(p * count + c, (p ^ 1) * count + c) for p in range(prompts) for c in range(count)]


def plane_pairs(prompts, step):
    count = SIDE * SIDE
    return [(p * count + c, (p + 2 * step) % prompts * count + c) for p in range(prompts) for c in range(count)]


def turned(meta_ref, k):
    return lax.rem(meta_ref[2] + k, SIDE)


def query_kernel(slot_ref, list_ref, used_ref, q_ref, sys_ref, far_ref, out_ref, tmp, sys_tmp):
    lane = lax.broadcasted_iota(jnp.int32, (16, HD), 1)
    flags = jnp.zeros((16, HD), F32)
    for n in range(64):
        slot = jnp.where(n < used_ref[0], slot_ref[0, list_ref[0, n]], -1)
        flags = jnp.where(lane == slot, 1.0, flags)
    for head in range(KVH):
        out = out_ref.at[head]
        for t in range(3):
            for g in range(GQ):
                at = pl.ds((head * GQ + g) * HD, HD)
                tmp[pl.ds(t * 64 + g * 4, 4), :] = q_ref[t, :, at].astype(F32)
        out[pl.ds(0, ROWS), :] = tmp[...].astype(BF)
        lanes = pl.ds(head * HD, HD)
        sys_tmp[pl.ds(0, SYS_PART), :] = sys_ref[:, :, lanes].reshape(SYS_PART, HD).astype(F32)
        sys_tmp[pl.ds(SYS_PART, SYS_PART), :] = far_ref[:, :, lanes].reshape(SYS_PART, HD).astype(F32)
        out[pl.ds(MSG, SYS_PART), :] = sys_tmp[pl.ds(0, SYS_PART, stride=2), :].astype(BF)
        out[pl.ds(MSG + SYS_PART, SYS_PART), :] = sys_tmp[pl.ds(1, SYS_PART, stride=2), :].astype(BF)
        out[pl.ds(ROWS, 16), :] = flags.astype(BF)


def stage_kernel(got_ref, stage_ref, sys_ref):
    for k in range(SIDE):
        stage_ref[k] = got_ref[k, pl.ds(0, MSG), :]
        for side in range(2):
            at = pl.ds(k * SYS_PART, SYS_PART)
            sys_ref[side, at, :] = got_ref[k, pl.ds(MSG + side * SYS_PART, SYS_PART), :]


def flatten_rows(lse):
    lane = lax.broadcasted_iota(jnp.int32, (BLK, HD), 1)
    row = lax.broadcasted_iota(jnp.int32, (BLK, HD), 0)
    rest = ROWS - BLK
    upper = jnp.sum(jnp.where(lane == row, lse[:BLK], 0.0), axis=0, keepdims=True)
    lower = jnp.sum(jnp.where((lane == row)[:rest], lse[BLK:], 0.0), axis=0, keepdims=True)
    return jnp.concatenate([upper, lower], axis=0)


def pack_flat(flat):
    hi = flat.astype(BF).astype(F32)
    mid = (flat - hi).astype(BF).astype(F32)
    low = flat - hi - mid
    return jnp.concatenate([hi, mid, low, jnp.zeros((10, HD), F32)], axis=0).astype(BF)


def unpack_flat(packed):
    wide = packed.astype(F32)
    return wide[0:2] + wide[2:4] + wide[4:6]


def weigh(flats):
    top = functools.reduce(jnp.maximum, flats)
    weights = [jnp.exp2(one - top) for one in flats]
    total = functools.reduce(jnp.add, weights)
    return [w / total for w in weights], top + jnp.log2(total)


def mix_all(weights, outs):
    flat = [w for group in weights for w in group]
    rows = 2 * len(flat)
    stacked = jnp.concatenate(flat + [jnp.zeros((HD - rows, HD), F32)], axis=0)
    columns = stacked.T
    mixed = []
    n = 0
    for group in outs:
        upper = lower = 0.0
        for one in group:
            upper = upper + columns[:, n : n + 1] * one[:BLK]
            lower = lower + columns[: ROWS - BLK, n + 1 : n + 2] * one[BLK:]
            n += 2
        mixed.append(jnp.concatenate([upper, lower], axis=0))
    return mixed


def main_kernel(meta_ref, owner_ref, *refs):
    q_refs, pool_ref, sys_refs, o_refs, refs = refs[:4], refs[4], refs[5:9], refs[9:13], refs[13:]
    kc, vc, bias, tmp, raw, sems = refs
    pair = 2 * ROWS
    copies = [pltpu.make_async_copy(pool_ref.at[k], raw.at[k], sems.at[k]) for k in range(SIDE)]
    for copy in copies:
        copy.start()

    def used_slots(prompt):
        column = lax.rem(meta_ref[0] - 2 * prompt + SIDE, SIDE)
        row = pl.ds(ROWS, 1)
        flags = q_refs[0][2 * prompt, row, :].astype(F32)
        for j in range(SIDE):
            chosen = (meta_ref[7] == 0) & (column == j)
            flags = jnp.where(chosen, q_refs[j][0, row, :].astype(F32), flags)
        return flags

    flags = [used_slots(0), used_slots(1)]
    lane = lax.broadcasted_iota(jnp.int32, (1, HD), 1)
    for p in range(2):
        vc[p, :, pl.ds(HD, HD)] = jnp.ones((ALL_TOK, HD), BF)
        for n in range(4):
            at = pl.ds(4 * POOL_TOK + n * BLK, BLK)
            kc[p, at, :] = sys_refs[n][0]
            vc[p, at, pl.ds(0, HD)] = sys_refs[n][1]
            bias[p, 16 + n] = jnp.zeros((8, HD), F32)
    for k in range(SIDE):
        copies[k].wait()
        held = tmp.at[k % 2]
        held[...] = raw[k].astype(F32)
        n0, n1 = jnp.int32(0), jnp.int32(0)
        for blk in range(8):
            slot = meta_ref[3 + k] + blk
            prompt = owner_ref[slot]
            rank = k * 4 + jnp.minimum(jnp.where(prompt == 0, n0, n1), 3)
            at = pl.ds(pl.multiple_of(rank * BLK, BLK), BLK)
            kc[prompt, at, :] = held[pl.ds(blk * 2 * BLK, BLK, stride=2), :].astype(BF)
            vc[prompt, at, pl.ds(0, HD)] = held[pl.ds(blk * 2 * BLK + 1, BLK, stride=2), :].astype(BF)
            live = jnp.where(prompt == 0, flags[0], flags[1])
            live = jnp.sum(jnp.where(lane == slot, live, 0.0), axis=1, keepdims=True)
            bias[prompt, rank] = jnp.broadcast_to((1.0 - live) * FLOOR, (8, HD))
            n0 = n0 + 1 - prompt
            n1 = n1 + prompt

    def prompt_of(i, n):
        row = lax.rem(meta_ref[0] - i + SIDE, SIDE)
        return jnp.where(meta_ref[7] == 0, row // 2, n)

    def scores(i, n):
        p = prompt_of(i, n)
        q = q_refs[i][2 * n : 2 * n + 2, :ROWS].reshape(pair, HD)
        s = lax.dot_general(q, kc[p], NT, preferred_element_type=F32)
        return s + jnp.concatenate([bias[p, t, :1, :] for t in range(20)], axis=1)

    def finish(i, n, s):
        m = jnp.max(s, axis=1, keepdims=True)
        w = jnp.exp2((s - m) * SCALE2).astype(BF)
        acc = jnp.dot(w, vc[prompt_of(i, n)], preferred_element_type=F32)
        total = acc[:, HD:]
        out = (acc[:, :HD] / total).astype(BF)
        lse = m * SCALE2 + jnp.log2(total)
        for half in range(2):
            part = slice(half * ROWS, (half + 1) * ROWS)
            o_refs[i][2 * n + half, pl.ds(0, ROWS), :] = out[part]
            o_refs[i][2 * n + half, pl.ds(ROWS, 16), :] = pack_flat(flatten_rows(lse[part]))

    jobs = [(i, n) for i in range(SIDE) for n in range(2)]
    s = scores(*jobs[0])
    for t, job in enumerate(jobs):
        following = scores(*jobs[t + 1]) if t + 1 < len(jobs) else None
        finish(*job, s)
        s = following


def own_kernel(lens_ref, q_ref, s0, s1, s2, s3, new_ref, o_ref, lse_ref, bias, tmp, vc):
    tokens = vc.shape[1]
    comp = lax.broadcasted_iota(jnp.int32, (ROWS, 256), 0) % 4
    place = lax.broadcasted_iota(jnp.int32, (ROWS, 256), 1)
    for c in range(4):
        live = (comp == c) & (place < lens_ref[c])
        bias[:, pl.ds(c * 256, 256)] = jnp.where(live, 0.0, FLOOR)
    row = lax.broadcasted_iota(jnp.int32, (ROWS, BLK), 0)
    col = lax.broadcasted_iota(jnp.int32, (ROWS, BLK), 1)
    fresh = col - (row % 4) * 3
    bias[:, pl.ds(1024, BLK)] = jnp.where((fresh >= 0) & (fresh < 3) & (fresh <= row // 64), 0.0, FLOOR)
    for n in range(2):
        vc[n, :, pl.ds(HD, HD)] = jnp.ones((tokens, HD), BF)
        tmp[n, pl.ds(2048, 256), :] = jnp.zeros((256, HD), F32)

    def scores(k, kv_ref):
        held = tmp.at[k % 2]
        held[pl.ds(0, 2048), :] = kv_ref[...].astype(F32)
        held[pl.ds(2048, 24), :] = new_ref[k].astype(F32)
        key = held[pl.ds(0, tokens, stride=2), :].astype(BF)
        vc[k % 2, :, pl.ds(0, HD)] = held[pl.ds(1, tokens, stride=2), :].astype(BF)
        s = lax.dot_general(q_ref[k, pl.ds(0, ROWS), :], key, NT, preferred_element_type=F32)
        return s + bias[...]

    def finish(k, s):
        m = jnp.max(s, axis=1, keepdims=True)
        w = jnp.exp2((s - m) * SCALE2).astype(BF)
        acc = jnp.dot(w, vc[k % 2], preferred_element_type=F32)
        total = acc[:, HD:]
        o_ref[k] = acc[:, :HD] / total
        lse_ref[k, pl.ds(0, 2), :] = flatten_rows(m * SCALE2 + jnp.log2(total))

    kv_refs = (s0, s1, s2, s3)
    s = scores(0, s0)
    for k in range(KVH):
        following = scores(k + 1, kv_refs[k + 1]) if k + 1 < KVH else None
        finish(k, s)
        s = following


def combine_kernel(meta_ref, c0, c1, c2, c3, o0, o1, o2, o3):
    parts = (c0, c1, c2, c3)
    weights, outs = [], []
    for k, out in enumerate((o0, o1, o2, o3)):
        n = turned(meta_ref, SIDE - k)
        group, lse = weigh([unpack_flat(ref[n, pl.ds(ROWS, 16), :]) for ref in parts])
        weights.append(group)
        outs.append([ref[n, pl.ds(0, ROWS), :].astype(F32) for ref in parts])
        out[pl.ds(ROWS, 16), :] = pack_flat(lse)
    for out, mixed in zip((o0, o1, o2, o3), mix_all(weights, outs)):
        out[pl.ds(0, ROWS), :] = mixed.astype(BF)


def final_kernel(meta_ref, r0, r1, r2, r3, own_ref, lse_ref, out_ref):
    refs = (r0, r1, r2, r3)
    heads = [turned(meta_ref, k) for k in range(KVH)]
    weights = [
        weigh([unpack_flat(ref[pl.ds(ROWS, 16), :]), lse_ref[head, pl.ds(0, 2), :]])[0]
        for head, ref in zip(heads, refs)
    ]
    outs = [[ref[pl.ds(0, ROWS), :].astype(F32), own_ref[head]] for head, ref in zip(heads, refs)]
    for head, mixed in zip(heads, mix_all(weights, outs)):
        for t in range(3):
            out_ref[t, head] = mixed[t * 64 : (t + 1) * 64].astype(BF)


def cost(flops, size, exps=0):
    return pl.CostEstimate(flops=flops, bytes_accessed=size, transcendentals=exps)


def shaped(shape, dtype=BF):
    return jax.ShapeDtypeStruct(shape, dtype)


def whole(array):
    return pl.BlockSpec(array.shape, lambda *_: (0,) * array.ndim)


def body(queries, new_kv, suffix_kv, suffix_len, pool_kv, sys_kv, block_slot, block_list, prefix_blocks):
    prompts = lax.axis_size("prompt")
    me_p = lax.axis_index("prompt")
    me_c = lax.axis_index("comp")
    y, x = me_c // SIDE, me_c % SIDE
    core = me_p % 2
    even = core == 0
    a = jnp.where(even, x, y)

    def send(array, role, step):
        return lax.ppermute(array, AXES, ring_pairs(prompts, role, step % SIDE))

    def source(n):
        return jnp.where(even, y * SIDE + n, n * SIDE + x) * 8

    meta = jnp.stack([y, x, a, source(0), source(1), source(2), source(3), core]).astype(jnp.int32)

    far_sys = lax.ppermute(sys_kv, AXES, core_pairs(prompts))

    def split_heads(array):
        return [array[..., h * HD : (h + 1) * HD].reshape(-1, HD) for h in range(KVH)]

    def exchange(array):
        return lax.all_to_all(array, AXES, 0, 0, axis_index_groups=ring_groups(prompts, "a"), tiled=True)

    by_head = jnp.stack(split_heads(pool_kv))

    q_msg = pl.pallas_call(
        query_kernel,
        in_specs=[SMEM] * 3 + [VMEM] * 3,
        out_specs=VMEM,
        out_shape=shaped((KVH, MSG + 2 * SYS_PART, HD)),
        scratch_shapes=[pltpu.VMEM((ROWS, HD), F32), pltpu.VMEM((2 * SYS_PART, HD), F32)],
        compiler_params=room(10),
        cost_estimate=cost(0, 2**19),
        name="query_messages",
    )(block_slot, block_list, prefix_blocks, queries.transpose(1, 0, 2), sys_kv, far_sys)
    q_got = exchange(q_msg)
    by_head, q_got = lax.optimization_barrier((by_head, q_got))
    pool = exchange(by_head)
    stage, sys_one = pl.pallas_call(
        stage_kernel,
        in_specs=[VMEM],
        out_specs=[VMEM] * 2,
        out_shape=[shaped((SIDE, MSG, HD)), shaped((2, BLK, HD))],
        compiler_params=room(8),
        cost_estimate=cost(0, 2**19),
        name="stage",
    )(q_got)
    columns = [stage] + [send(stage, "b", j) for j in (1, 2, 3)]
    system = [sys_one] + [lax.ppermute(sys_one, AXES, plane_pairs(prompts, k)) for k in (1, 2, 3)]

    places = jnp.arange(128, dtype=jnp.int32)
    owner = jnp.sum(jnp.where((block_slot[0][:, None] == places) & (places[:, None] >= 64), 1, 0), axis=0)

    parts = pl.pallas_call(
        main_kernel,
        grid_spec=pltpu.PrefetchScalarGridSpec(
            num_scalar_prefetch=2,
            grid=(1,),
            in_specs=[whole(one) for one in columns] + [pl.BlockSpec(memory_space=pl.ANY)] + [whole(sys_one)] * 4,
            out_specs=[pl.BlockSpec((SIDE, MSG, HD), lambda *_: (0, 0, 0))] * SIDE,
            scratch_shapes=[
                pltpu.VMEM((2, ALL_TOK, HD), BF),
                pltpu.VMEM((2, ALL_TOK, 2 * HD), BF),
                pltpu.VMEM((2, 20, 8, HD), F32),
                pltpu.VMEM((2, 2048, HD), F32),
                pltpu.VMEM((SIDE, 2048, HD), BF),
                pltpu.SemaphoreType.DMA((SIDE,)),
            ],
        ),
        out_shape=[shaped((SIDE, MSG, HD))] * SIDE,
        compiler_params=room(38),
        cost_estimate=cost(2**33, 2**22, 2**23),
        name="attend",
    )(meta, owner, *columns, pool, *system)
    parts = list(parts)
    parts = [parts[0]] + [send(parts[j], "b", -j) for j in (1, 2, 3)]
    suffix_len, parts[0] = lax.optimization_barrier((suffix_len, parts[0]))
    new_heads = jnp.stack(split_heads(new_kv))
    own_out, own_lse = pl.pallas_call(
        own_kernel,
        in_specs=[SMEM] + [VMEM] * 6,
        out_specs=[VMEM] * 2,
        out_shape=[shaped((KVH, ROWS, HD), F32), shaped((KVH, 8, HD), F32)],
        scratch_shapes=[
            pltpu.VMEM((ROWS, 1024 + BLK), F32),
            pltpu.VMEM((2, 2048 + 2 * BLK, HD), F32),
            pltpu.VMEM((2, 1024 + BLK, 2 * HD), BF),
        ],
        compiler_params=room(20),
        cost_estimate=cost(2**30, 2**22, 2**20),
        name="own_tokens",
    )(suffix_len, q_msg, *split_heads(suffix_kv), new_heads)
    back = pl.pallas_call(
        combine_kernel,
        in_specs=[SMEM] + [VMEM] * 4,
        out_specs=[VMEM] * 4,
        out_shape=[shaped((MSG, HD))] * 4,
        compiler_params=room(10),
        cost_estimate=cost(0, 2**20),
        name="combine",
    )(meta, *parts)
    heads = [back[0]] + [send(back[k], "a", -k) for k in (1, 2, 3)]
    out = pl.pallas_call(
        final_kernel,
        in_specs=[SMEM] + [VMEM] * 6,
        out_specs=VMEM,
        out_shape=shaped((3, KVH, 64, HD)),
        compiler_params=room(10),
        name="final",
    )(meta, *heads, own_out, own_lse)
    return out.reshape(3, KVH, GQ, 4, HD).transpose(3, 0, 1, 2, 4).reshape(4, 3, QH * HD)


def solution(mesh):
    both = P(AXES)
    in_specs = (both,) * 6 + (P("prompt"), both, both)
    return jax.shard_map(body, mesh=mesh, in_specs=in_specs, out_specs=both, check_vma=False)
```

```python
import functools

import jax
import jax.numpy as jnp
from jax import lax
from jax.experimental import pallas as pl
from jax.experimental.pallas import tpu as pltpu
from jax.sharding import PartitionSpec as P

QH = 64
KVH = 4
HD = 128
GQ = QH // KVH
SIDE = 4
BLK = 128
ROWS = 192
MSG = ROWS + 16
SYS_PART = 32
POOL_TOK = 512
ALL_TOK = 5 * POOL_TOK
AXES = ("prompt", "comp")
FLOOR = -1e30
SCALE2 = HD**-0.5 * 1.4426950408889634
BF = jnp.bfloat16
F32 = jnp.float32
NT = (((1,), (1,)), ((), ()))


def room(mib):
    return pltpu.CompilerParams(vmem_limit_bytes=mib * 2**20)


SMEM = pl.BlockSpec(memory_space=pltpu.SMEM)
VMEM = pl.BlockSpec(memory_space=pltpu.VMEM)


def ring_pairs(prompts, role, step):
    pairs = []
    for p in range(prompts):
        along_x = (p % 2 == 0) == (role == "a")
        for y in range(SIDE):
            for x in range(SIDE):
                ty = y if along_x else (y + step) % SIDE
                tx = (x + step) % SIDE if along_x else x
                base = p * SIDE * SIDE
                pairs.append((base + y * SIDE + x, base + ty * SIDE + tx))
    return pairs


def ring_groups(prompts, role):
    step = ring_pairs(prompts, role, 1)
    follow = dict(step)
    groups = []
    for p in range(prompts):
        along_x = (p % 2 == 0) == (role == "a")
        for n in range(SIDE):
            group = [p * SIDE * SIDE + (n * SIDE if along_x else n)]
            while len(group) < SIDE:
                group.append(follow[group[-1]])
            groups.append(group)
    return groups


def core_pairs(prompts):
    count = SIDE * SIDE
    return [(p * count + c, (p ^ 1) * count + c) for p in range(prompts) for c in range(count)]


def plane_pairs(prompts, step):
    count = SIDE * SIDE
    return [(p * count + c, (p + 2 * step) % prompts * count + c) for p in range(prompts) for c in range(count)]


def turned(meta_ref, k):
    return lax.rem(meta_ref[2] + k, SIDE)


def query_kernel(meta_ref, slot_ref, list_ref, used_ref, q_ref, sys_ref, far_ref, o0, o1, o2, o3, tmp, sys_tmp):
    lane = lax.broadcasted_iota(jnp.int32, (16, HD), 1)
    flags = jnp.zeros((16, HD), F32)
    for n in range(64):
        slot = jnp.where(n < used_ref[0], slot_ref[0, list_ref[0, n]], -1)
        flags = jnp.where(lane == slot, 1.0, flags)
    for k, out in enumerate((o0, o1, o2, o3)):
        head = turned(meta_ref, k)
        for t in range(3):
            for g in range(GQ):
                at = pl.ds(pl.multiple_of((head * GQ + g) * HD, HD), HD)
                tmp[pl.ds(t * 64 + g * 4, 4), :] = q_ref[t, :, at].astype(F32)
        out[pl.ds(0, ROWS), :] = tmp[...].astype(BF)
        lanes = pl.ds(pl.multiple_of(head * HD, HD), HD)
        sys_tmp[pl.ds(0, SYS_PART), :] = sys_ref[:, :, lanes].reshape(SYS_PART, HD).astype(F32)
        sys_tmp[pl.ds(SYS_PART, SYS_PART), :] = far_ref[:, :, lanes].reshape(SYS_PART, HD).astype(F32)
        out[pl.ds(MSG, SYS_PART), :] = sys_tmp[pl.ds(0, SYS_PART, stride=2), :].astype(BF)
        out[pl.ds(MSG + SYS_PART, SYS_PART), :] = sys_tmp[pl.ds(1, SYS_PART, stride=2), :].astype(BF)
        out[pl.ds(ROWS, 16), :] = flags.astype(BF)


def stage_kernel(meta_ref, m0, m1, m2, m3, stage_ref, sys_ref):
    for k, msg in enumerate((m0, m1, m2, m3)):
        stage_ref[turned(meta_ref, SIDE - k)] = msg[pl.ds(0, MSG), :]
        for side in range(2):
            at = pl.ds(k * SYS_PART, SYS_PART)
            sys_ref[side, at, :] = msg[pl.ds(MSG + side * SYS_PART, SYS_PART), :]


def head_kernel(pool_ref, out_ref, sems):
    copies = [
        pltpu.make_async_copy(pool_ref.at[:, :, :, pl.ds(h * HD, HD)], out_ref.at[h], sems.at[h]) for h in range(KVH)
    ]
    for copy in copies:
        copy.start()
    for copy in copies:
        copy.wait()


def flatten_rows(lse):
    lane = lax.broadcasted_iota(jnp.int32, (BLK, HD), 1)
    row = lax.broadcasted_iota(jnp.int32, (BLK, HD), 0)
    rest = ROWS - BLK
    upper = jnp.sum(jnp.where(lane == row, lse[:BLK], 0.0), axis=0, keepdims=True)
    lower = jnp.sum(jnp.where((lane == row)[:rest], lse[BLK:], 0.0), axis=0, keepdims=True)
    return jnp.concatenate([upper, lower], axis=0)


def pack_flat(flat):
    hi = flat.astype(BF).astype(F32)
    mid = (flat - hi).astype(BF).astype(F32)
    low = flat - hi - mid
    return jnp.concatenate([hi, mid, low, jnp.zeros((10, HD), F32)], axis=0).astype(BF)


def unpack_flat(packed):
    wide = packed.astype(F32)
    return wide[0:2] + wide[2:4] + wide[4:6]


def weigh(flats):
    top = functools.reduce(jnp.maximum, flats)
    weights = [jnp.exp2(one - top) for one in flats]
    total = functools.reduce(jnp.add, weights)
    return [w / total for w in weights], top + jnp.log2(total)


def mix_all(weights, outs):
    flat = [w for group in weights for w in group]
    rows = 2 * len(flat)
    stacked = jnp.concatenate(flat + [jnp.zeros((HD - rows, HD), F32)], axis=0)
    columns = stacked.T
    mixed = []
    n = 0
    for group in outs:
        upper = lower = 0.0
        for one in group:
            upper = upper + columns[:, n : n + 1] * one[:BLK]
            lower = lower + columns[: ROWS - BLK, n + 1 : n + 2] * one[BLK:]
            n += 2
        mixed.append(jnp.concatenate([upper, lower], axis=0))
    return mixed


def main_kernel(meta_ref, owner_ref, *refs):
    q_refs, pool_ref, sys_refs, o_refs, refs = refs[:4], refs[4], refs[5:9], refs[9:13], refs[13:]
    kc, vc, bias, tmp, raw, sems = refs
    pair = 2 * ROWS
    copies = [pltpu.make_async_copy(pool_ref.at[k], raw.at[k], sems.at[k]) for k in range(SIDE)]
    for copy in copies:
        copy.start()

    def used_slots(prompt):
        column = lax.rem(meta_ref[0] - 2 * prompt + SIDE, SIDE)
        row = pl.ds(ROWS, 1)
        flags = q_refs[0][2 * prompt, row, :].astype(F32)
        for j in range(SIDE):
            chosen = (meta_ref[7] == 0) & (column == j)
            flags = jnp.where(chosen, q_refs[j][0, row, :].astype(F32), flags)
        return flags

    flags = [used_slots(0), used_slots(1)]
    lane = lax.broadcasted_iota(jnp.int32, (1, HD), 1)
    for p in range(2):
        vc[p, :, pl.ds(HD, HD)] = jnp.ones((ALL_TOK, HD), BF)
        for n in range(4):
            at = pl.ds(4 * POOL_TOK + n * BLK, BLK)
            kc[p, at, :] = sys_refs[n][0]
            vc[p, at, pl.ds(0, HD)] = sys_refs[n][1]
            bias[p, 16 + n] = jnp.zeros((8, HD), F32)
    for k in range(SIDE):
        copies[k].wait()
        held = tmp.at[k % 2]
        held[...] = raw[k].astype(F32)
        n0, n1 = jnp.int32(0), jnp.int32(0)
        for blk in range(8):
            slot = meta_ref[3 + k] + blk
            prompt = owner_ref[slot]
            rank = k * 4 + jnp.minimum(jnp.where(prompt == 0, n0, n1), 3)
            at = pl.ds(pl.multiple_of(rank * BLK, BLK), BLK)
            kc[prompt, at, :] = held[pl.ds(blk * 2 * BLK, BLK, stride=2), :].astype(BF)
            vc[prompt, at, pl.ds(0, HD)] = held[pl.ds(blk * 2 * BLK + 1, BLK, stride=2), :].astype(BF)
            live = jnp.where(prompt == 0, flags[0], flags[1])
            live = jnp.sum(jnp.where(lane == slot, live, 0.0), axis=1, keepdims=True)
            bias[prompt, rank] = jnp.broadcast_to((1.0 - live) * FLOOR, (8, HD))
            n0 = n0 + 1 - prompt
            n1 = n1 + prompt

    def prompt_of(i, n):
        row = lax.rem(meta_ref[0] - i + SIDE, SIDE)
        return jnp.where(meta_ref[7] == 0, row // 2, n)

    def scores(i, n):
        p = prompt_of(i, n)
        q = q_refs[i][2 * n : 2 * n + 2, :ROWS].reshape(pair, HD)
        s = lax.dot_general(q, kc[p], NT, preferred_element_type=F32)
        return s + jnp.concatenate([bias[p, t, :1, :] for t in range(20)], axis=1)

    def finish(i, n, s):
        m = jnp.max(s, axis=1, keepdims=True)
        w = jnp.exp2((s - m) * SCALE2).astype(BF)
        acc = jnp.dot(w, vc[prompt_of(i, n)], preferred_element_type=F32)
        total = acc[:, HD:]
        out = (acc[:, :HD] / total).astype(BF)
        lse = m * SCALE2 + jnp.log2(total)
        for half in range(2):
            part = slice(half * ROWS, (half + 1) * ROWS)
            o_refs[i][2 * n + half, pl.ds(0, ROWS), :] = out[part]
            o_refs[i][2 * n + half, pl.ds(ROWS, 16), :] = pack_flat(flatten_rows(lse[part]))

    jobs = [(i, n) for i in range(SIDE) for n in range(2)]
    s = scores(*jobs[0])
    for t, job in enumerate(jobs):
        following = scores(*jobs[t + 1]) if t + 1 < len(jobs) else None
        finish(*job, s)
        s = following


def own_kernel(lens_ref, q0, q1, q2, q3, s0, s1, s2, s3, new_ref, o_ref, lse_ref, bias, tmp, vc):
    tokens = vc.shape[1]
    comp = lax.broadcasted_iota(jnp.int32, (ROWS, 256), 0) % 4
    place = lax.broadcasted_iota(jnp.int32, (ROWS, 256), 1)
    for c in range(4):
        live = (comp == c) & (place < lens_ref[c])
        bias[:, pl.ds(c * 256, 256)] = jnp.where(live, 0.0, FLOOR)
    row = lax.broadcasted_iota(jnp.int32, (ROWS, BLK), 0)
    col = lax.broadcasted_iota(jnp.int32, (ROWS, BLK), 1)
    fresh = col - (row % 4) * 3
    bias[:, pl.ds(1024, BLK)] = jnp.where((fresh >= 0) & (fresh < 3) & (fresh <= row // 64), 0.0, FLOOR)
    for n in range(2):
        vc[n, :, pl.ds(HD, HD)] = jnp.ones((tokens, HD), BF)
        tmp[n, pl.ds(2048, 256), :] = jnp.zeros((256, HD), F32)

    def scores(k, q_ref, kv_ref):
        held = tmp.at[k % 2]
        held[pl.ds(0, 2048), :] = kv_ref[...].astype(F32)
        held[pl.ds(2048, 24), :] = new_ref[k].astype(F32)
        key = held[pl.ds(0, tokens, stride=2), :].astype(BF)
        vc[k % 2, :, pl.ds(0, HD)] = held[pl.ds(1, tokens, stride=2), :].astype(BF)
        s = lax.dot_general(q_ref[pl.ds(0, ROWS), :], key, NT, preferred_element_type=F32)
        return s + bias[...]

    def finish(k, s):
        m = jnp.max(s, axis=1, keepdims=True)
        w = jnp.exp2((s - m) * SCALE2).astype(BF)
        acc = jnp.dot(w, vc[k % 2], preferred_element_type=F32)
        total = acc[:, HD:]
        o_ref[k] = acc[:, :HD] / total
        lse_ref[k, pl.ds(0, 2), :] = flatten_rows(m * SCALE2 + jnp.log2(total))

    q_refs, kv_refs = (q0, q1, q2, q3), (s0, s1, s2, s3)
    s = scores(0, q0, s0)
    for k in range(KVH):
        following = scores(k + 1, q_refs[k + 1], kv_refs[k + 1]) if k + 1 < KVH else None
        finish(k, s)
        s = following


def combine_kernel(meta_ref, c0, c1, c2, c3, o0, o1, o2, o3):
    parts = (c0, c1, c2, c3)
    weights, outs = [], []
    for k, out in enumerate((o0, o1, o2, o3)):
        n = turned(meta_ref, SIDE - k)
        group, lse = weigh([unpack_flat(ref[n, pl.ds(ROWS, 16), :]) for ref in parts])
        weights.append(group)
        outs.append([ref[n, pl.ds(0, ROWS), :].astype(F32) for ref in parts])
        out[pl.ds(ROWS, 16), :] = pack_flat(lse)
    for out, mixed in zip((o0, o1, o2, o3), mix_all(weights, outs)):
        out[pl.ds(0, ROWS), :] = mixed.astype(BF)


def final_kernel(meta_ref, r0, r1, r2, r3, own_ref, lse_ref, out_ref):
    refs = (r0, r1, r2, r3)
    weights = [
        weigh([unpack_flat(ref[pl.ds(ROWS, 16), :]), lse_ref[k, pl.ds(0, 2), :]])[0] for k, ref in enumerate(refs)
    ]
    outs = [[ref[pl.ds(0, ROWS), :].astype(F32), own_ref[k]] for k, ref in enumerate(refs)]
    for k, mixed in enumerate(mix_all(weights, outs)):
        head = turned(meta_ref, k)
        for t in range(3):
            out_ref[t, head] = mixed[t * 64 : (t + 1) * 64].astype(BF)


def cost(flops, size, exps=0):
    return pl.CostEstimate(flops=flops, bytes_accessed=size, transcendentals=exps)


def shaped(shape, dtype=BF):
    return jax.ShapeDtypeStruct(shape, dtype)


def whole(array):
    return pl.BlockSpec(array.shape, lambda *_: (0,) * array.ndim)


def body(queries, new_kv, suffix_kv, suffix_len, pool_kv, sys_kv, block_slot, block_list, prefix_blocks):
    prompts = lax.axis_size("prompt")
    me_p = lax.axis_index("prompt")
    me_c = lax.axis_index("comp")
    y, x = me_c // SIDE, me_c % SIDE
    core = me_p % 2
    even = core == 0
    a = jnp.where(even, x, y)

    def send(array, role, step):
        return lax.ppermute(array, AXES, ring_pairs(prompts, role, step % SIDE))

    def source(n):
        return jnp.where(even, y * SIDE + n, n * SIDE + x) * 8

    meta = jnp.stack([y, x, a, source(0), source(1), source(2), source(3), core]).astype(jnp.int32)

    far_sys = lax.ppermute(sys_kv, AXES, core_pairs(prompts))

    def one_head(array, k):
        return lax.dynamic_slice_in_dim(array, ((a + k) % SIDE) * HD, HD, array.ndim - 1).reshape(-1, HD)

    by_head = pl.pallas_call(
        head_kernel,
        in_specs=[pl.BlockSpec(memory_space=pltpu.HBM)],
        out_specs=pl.BlockSpec(memory_space=pl.ANY),
        out_shape=shaped((KVH, *pool_kv.shape[:3], HD)),
        scratch_shapes=[pltpu.SemaphoreType.DMA((KVH,))],
        compiler_params=room(4),
        cost_estimate=cost(0, 2**22),
        name="split_heads",
    )(pool_kv).reshape(KVH, -1, HD)
    by_head, far_sys = lax.optimization_barrier((by_head, far_sys))

    q_msgs = pl.pallas_call(
        query_kernel,
        in_specs=[SMEM] * 4 + [VMEM] * 3,
        out_specs=[VMEM] * 4,
        out_shape=[shaped((MSG + 2 * SYS_PART, HD))] * 4,
        scratch_shapes=[pltpu.VMEM((ROWS, HD), F32), pltpu.VMEM((2 * SYS_PART, HD), F32)],
        compiler_params=room(10),
        cost_estimate=cost(0, 2**19),
        name="query_messages",
    )(meta, block_slot, block_list, prefix_blocks, queries.transpose(1, 0, 2), sys_kv, far_sys)
    q_got = [q_msgs[0]] + [send(q_msgs[k], "a", k) for k in (1, 2, 3)]
    by_head, *q_got = lax.optimization_barrier((by_head, *q_got))
    pool = lax.all_to_all(by_head, AXES, 0, 0, axis_index_groups=ring_groups(prompts, "a"), tiled=True)
    stage, sys_one = pl.pallas_call(
        stage_kernel,
        in_specs=[SMEM] + [VMEM] * 4,
        out_specs=[VMEM] * 2,
        out_shape=[shaped((SIDE, MSG, HD)), shaped((2, BLK, HD))],
        compiler_params=room(8),
        cost_estimate=cost(0, 2**19),
        name="stage",
    )(meta, *q_got)
    columns = [stage] + [send(stage, "b", j) for j in (1, 2, 3)]
    system = [sys_one] + [lax.ppermute(sys_one, AXES, plane_pairs(prompts, k)) for k in (1, 2, 3)]

    places = jnp.arange(128, dtype=jnp.int32)
    owner = jnp.sum(jnp.where((block_slot[0][:, None] == places) & (places[:, None] >= 64), 1, 0), axis=0)

    parts = pl.pallas_call(
        main_kernel,
        grid_spec=pltpu.PrefetchScalarGridSpec(
            num_scalar_prefetch=2,
            grid=(1,),
            in_specs=[whole(one) for one in columns] + [pl.BlockSpec(memory_space=pl.ANY)] + [whole(sys_one)] * 4,
            out_specs=[pl.BlockSpec((SIDE, MSG, HD), lambda *_: (0, 0, 0))] * SIDE,
            scratch_shapes=[
                pltpu.VMEM((2, ALL_TOK, HD), BF),
                pltpu.VMEM((2, ALL_TOK, 2 * HD), BF),
                pltpu.VMEM((2, 20, 8, HD), F32),
                pltpu.VMEM((2, 2048, HD), F32),
                pltpu.VMEM((SIDE, 2048, HD), BF),
                pltpu.SemaphoreType.DMA((SIDE,)),
            ],
        ),
        out_shape=[shaped((SIDE, MSG, HD))] * SIDE,
        compiler_params=room(38),
        cost_estimate=cost(2**33, 2**22, 2**23),
        name="attend",
    )(meta, owner, *columns, pool, *system)
    parts = list(parts)
    parts = [parts[0]] + [send(parts[j], "b", -j) for j in (1, 2, 3)]
    suffix_len, parts[0] = lax.optimization_barrier((suffix_len, parts[0]))
    new_heads = jnp.stack([one_head(new_kv, k) for k in range(KVH)])
    own_out, own_lse = pl.pallas_call(
        own_kernel,
        in_specs=[SMEM] + [VMEM] * 9,
        out_specs=[VMEM] * 2,
        out_shape=[shaped((KVH, ROWS, HD), F32), shaped((KVH, 8, HD), F32)],
        scratch_shapes=[
            pltpu.VMEM((ROWS, 1024 + BLK), F32),
            pltpu.VMEM((2, 2048 + 2 * BLK, HD), F32),
            pltpu.VMEM((2, 1024 + BLK, 2 * HD), BF),
        ],
        compiler_params=room(20),
        cost_estimate=cost(2**30, 2**22, 2**20),
        name="own_tokens",
    )(suffix_len, *q_msgs, *[one_head(suffix_kv, k) for k in range(KVH)], new_heads)
    back = pl.pallas_call(
        combine_kernel,
        in_specs=[SMEM] + [VMEM] * 4,
        out_specs=[VMEM] * 4,
        out_shape=[shaped((MSG, HD))] * 4,
        compiler_params=room(10),
        cost_estimate=cost(0, 2**20),
        name="combine",
    )(meta, *parts)
    heads = [back[0]] + [send(back[k], "a", -k) for k in (1, 2, 3)]
    out = pl.pallas_call(
        final_kernel,
        in_specs=[SMEM] + [VMEM] * 6,
        out_specs=VMEM,
        out_shape=shaped((3, KVH, 64, HD)),
        compiler_params=room(10),
        name="final",
    )(meta, *heads, own_out, own_lse)
    return out.reshape(3, KVH, GQ, 4, HD).transpose(3, 0, 1, 2, 4).reshape(4, 3, QH * HD)


def solution(mesh):
    both = P(AXES)
    in_specs = (both,) * 6 + (P("prompt"), both, both)
    return jax.shard_map(body, mesh=mesh, in_specs=in_specs, out_specs=both, check_vma=False)
```
